512 devices in a mesh: dp: 32 (over z, core), expert: 16 (over y, x).
Axes of the slice: x: 4, y: 4, z: 16, core: 2. Of those that a mesh axis runs over, the one named last changes fastest.
Arguments:
- tokens: bfloat16 [65536, 2048], P(('dp', 'expert')), may hold values from -6 to 6
- routes: int32 [65536, 2], P(('dp', 'expert')), may hold values from 0 to 15, all different within a row; in each aligned block of 128 rows (0 to 127, 128 to 255, ...) at most 18 rows name the same one
- gates: float32 [65536, 2], P(('dp', 'expert')), may hold values from 0.2 to 1
- cotangent: bfloat16 [65536, 2048], P(('dp', 'expert')), may hold values from -6 to 6
- up_weight: bfloat16 [16, 2048, 384], P('expert', 'dp'), may hold values from -0.125 to 0.125
- down_weight: bfloat16 [16, 2048, 384], P('expert', 'dp'), may hold values from -0.3125 to 0.3125
Outputs:
- mixed: bfloat16 [65536, 2048], P(('dp', 'expert'))
- input_grad: bfloat16 [65536, 2048], P(('dp', 'expert'))
- up_grad: bfloat16 [16, 2048, 384], P('expert', 'dp')
- down_grad: bfloat16 [16, 2048, 384], P('expert', 'dp')
The draws below stay inside these ranges and needn't reach their ends.
Inputs may be any that keep to these rules, and one draw needn't show every extreme that they name: `routes`: each row names two different experts; in each device's block of 128 rows no expert is named by more than 18 rows, a bound that some block reaches.
All inputs are finite; a program needn't handle non-finite values.
Results may differ from the reference program's by a relative error of at most 0.03.
Values may be sent and summed in bfloat16 or wider, within the bound.
No kernel may reach another device: no remote copies, remote signals or barrier semaphores. Data moves between devices by JAX's collectives and lax.ppermute only.
A program may use at most 64 MiB of HBM per device.

```python
import math
import jax
import jax.numpy as jnp
import numpy as np
from jax import lax

D = 2048
H = 384
TOK_DEV = 128
EXPERTS = 16
CAP = 18
TOKENS = 65536
N_DP = 32


def levels(rng, dims, cuts, least, high):
    factor_of = 1.0
    for position, blocks in cuts:
        heights = jax.random.uniform(jax.random.fold_in(jax.random.fold_in(rng, 6), position), (blocks,), jnp.float32, least / len(cuts), high / len(cuts))
        factor_of = factor_of * jnp.repeat(jnp.exp(heights), dims[position] // blocks).reshape((-1,) + (1,) * (len(dims) - 1 - position))
    return factor_of


def routed_block(key, own, number, rows, amount, top, most, slope):
    sequence = jax.random.permutation(key, amount)
    heavy_load, ordinary = portions_of(amount, rows * top, most, slope, True), portions_of(amount, rows * top, most, slope, False)
    places = jnp.arange(amount)

    def named(lengths, rotation):
        used = int((lengths > 0).sum())
        fixed = max(1, used // 4)
        moved = fixed + (places - fixed + rotation * (used - fixed)) % max(1, amount - fixed)
        return jnp.zeros((amount,), jnp.int32).at[sequence[jnp.where(places < fixed, places, moved)]].set(jnp.asarray(lengths, jnp.int32))

    lengths = jnp.where(number % 4 == 0, named(heavy_load, number // 4), named(ordinary, number - number // 4 - 1))
    mixed = jax.random.permutation(jax.random.fold_in(own, 3), amount)
    source_of, receiver = mixed[0:amount // 2 * 2:2], mixed[1:amount // 2 * 2:2]
    room = jnp.minimum(lengths[source_of] - 1, most - lengths[receiver]) // 2
    room = jnp.where((source_of == sequence[0]) | (receiver == sequence[0]) | (lengths[receiver] == 0), 0, jnp.maximum(room, 0))
    moved = jax.random.randint(jax.random.fold_in(own, 4), (amount // 2,), 0, 1 << 20) % (room + 1)
    lengths = lengths.at[source_of].add(-moved).at[receiver].add(moved)
    labels = jnp.searchsorted(jnp.cumsum(lengths), jnp.arange(rows * top), side="right").astype(jnp.int32)
    table = labels.reshape(top, rows).T
    table = table[jax.random.permutation(jax.random.fold_in(own, 1), rows)]
    rotation = jax.random.randint(jax.random.fold_in(own, 2), (rows, 1), 0, top)
    return jnp.take_along_axis(table, (jnp.arange(top)[None, :] + rotation) % top, axis=1)


def portions_of(amount, total, bound, lean, full):
    loads = [(1 << 20) // math.isqrt(rank ** lean) + 1 for rank in range(1, amount + 1)]
    largest = bound if full else min(bound, max(-(-total // amount), total * loads[0] // sum(loads)))
    least = 1 if total - largest >= amount - 1 else 0
    holding, surplus = [largest] + [least] * (amount - 1), total - largest - least * (amount - 1)
    while surplus > 0:
        candidates = [i for i in range(1, amount) if holding[i] < largest] or [i for i in range(1, amount) if holding[i] < bound]
        whole, remaining = sum([loads[i] for i in candidates]), surplus
        for i in candidates:
            extra = min(bound - holding[i], max(1, remaining * loads[i] // whole), surplus)
            holding[i] = holding[i] + extra
            surplus = surplus - extra
    return np.array(holding)


def bell_draw(key, shape, scale, reach, cuts=(), held_as=jnp.bfloat16):
    entries = jax.random.normal(key, shape, jnp.float32) * scale
    if len(cuts) > 0:
        entries = levels(key, shape, cuts, -0.22, 0.18) * entries
    return jnp.clip(entries, min=-reach, max=reach).astype(held_as)


def setup_inputs(seed: int = 0) -> dict:
    splits = jax.random.split(jax.random.key(seed), 7)
    tokens = bell_draw(splits[0], (TOKENS, D), 1.0, 6.0, ((0, 512),))
    routes_keys = jax.random.split(jax.random.fold_in(splits[1], 1), TOKENS // TOK_DEV)
    routes_turns = jax.random.permutation(jax.random.fold_in(splits[1], 3), TOKENS // TOK_DEV)
    routes = jax.vmap(lambda own, number: routed_block(jax.random.fold_in(splits[1], 2), own, number, TOK_DEV, EXPERTS, 2, CAP, 2))(routes_keys, routes_turns).reshape((TOKENS, 2))
    gates = jnp.clip(0.2 + 0.8 * jax.random.uniform(splits[2], (TOKENS, 2), jnp.float32) ** levels(splits[2], (TOKENS, 2), ((0, 512),), -0.2, 0.2), 0.2, 1.0)
    cotangent = bell_draw(splits[3], (TOKENS, D), 1.0, 6.0, ((0, 512),))
    up_weight = bell_draw(splits[4], (EXPERTS, D, H), D ** -0.5, 0.125, ((0, 16), (1, 32)))
    down_weight = bell_draw(splits[5], (EXPERTS, D, H), H ** -0.5, 0.3125, ((0, 16), (1, 32)))
    return {"tokens": tokens, "routes": routes, "gates": gates, "cotangent": cotangent, "up_weight": up_weight, "down_weight": down_weight}


def slot_of(block_routes):
    flat = block_routes.reshape(-1).astype(jnp.int32)
    onehot = (flat[:, None] == jnp.arange(EXPERTS, dtype=jnp.int32)[None, :]).astype(jnp.int32)
    earlier = jnp.cumsum(onehot, axis=0) - onehot
    return flat, jnp.sum(earlier * onehot, axis=1).astype(jnp.int32)


def reference(tokens, routes, gates, cotangent, up_weight, down_weight):
    width = tokens.shape[1]
    hidden = up_weight.shape[2]
    group_rows = EXPERTS * CAP
    tok_g = tokens.reshape(N_DP, EXPERTS, TOK_DEV, width)
    route_g = routes.reshape(N_DP, EXPERTS, TOK_DEV, 2)
    gate_g = gates.reshape(N_DP, EXPERTS, TOK_DEV, 2)
    cot_g = cotangent.reshape(N_DP, EXPERTS, TOK_DEV, width)
    up_full = up_weight.astype(jnp.float32)
    down_full = down_weight.astype(jnp.float32)

    def one_group(carry, inputs):
        tok, route, gate, cot = inputs
        flat, slot = jax.vmap(slot_of)(route)
        source = jnp.arange(EXPERTS, dtype=jnp.int32)[:, None]
        where = (flat * (EXPERTS * CAP) + source * CAP + slot).astype(jnp.int32).reshape(-1)
        pair_x = jnp.broadcast_to(tok[:, :, None, :], (EXPERTS, TOK_DEV, 2, width)).reshape(-1, width)
        pair_do = (gate[..., None] * cot[:, :, None, :].astype(jnp.float32)).astype(jnp.bfloat16).reshape(-1, width)
        xb = jnp.zeros((EXPERTS * group_rows, width), tokens.dtype).at[where].set(pair_x)
        dob = jnp.zeros((EXPERTS * group_rows, width), pair_do.dtype).at[where].set(pair_do)
        xb = xb.reshape(EXPERTS, group_rows, width).astype(jnp.float32)
        dob = dob.reshape(EXPERTS, group_rows, width).astype(jnp.float32)
        hpre = jnp.einsum('esd,edh->esh', xb, up_full)
        act = jax.nn.silu(hpre).astype(jnp.bfloat16)
        outb = jnp.einsum('esh,edh->esd', act.astype(jnp.float32), down_full).astype(jnp.bfloat16)
        dact = jnp.einsum('esd,edh->esh', dob, down_full)
        sig = jax.nn.sigmoid(hpre)
        dh = (dact * sig * (1.0 + hpre * (1.0 - sig))).astype(jnp.bfloat16)
        dxb = jnp.einsum('esh,edh->esd', dh.astype(jnp.float32), up_full).astype(jnp.bfloat16)
        up_part = jnp.einsum('esd,esh->edh', xb, dh.astype(jnp.float32)).astype(jnp.bfloat16)
        down_part = jnp.einsum('esd,esh->edh', dob, act.astype(jnp.float32)).astype(jnp.bfloat16)
        out_pairs = outb.reshape(-1, width)[where].astype(jnp.float32).reshape(EXPERTS, TOK_DEV, 2, width)
        mixed = jnp.sum(gate[..., None] * out_pairs, axis=2).astype(jnp.bfloat16)
        dx_pairs = dxb.reshape(-1, width)[where].astype(jnp.float32).reshape(EXPERTS, TOK_DEV, 2, width)
        input_grad = jnp.sum(dx_pairs, axis=2).astype(jnp.bfloat16)
        carry = (carry[0] + up_part.astype(jnp.float32), carry[1] + down_part.astype(jnp.float32))
        return carry, (mixed, input_grad)

    start = (jnp.zeros((EXPERTS, width, hidden), jnp.float32), jnp.zeros((EXPERTS, width, hidden), jnp.float32))
    sums, outs = lax.scan(one_group, start, (tok_g, route_g, gate_g, cot_g))
    mixed = outs[0].reshape(-1, width)
    input_grad = outs[1].reshape(-1, width)
    return mixed, input_grad, sums[0].astype(jnp.bfloat16), sums[1].astype(jnp.bfloat16)
```

```python
import functools

import jax
import jax.numpy as jnp
from jax import lax
from jax.experimental import pallas as pl
from jax.experimental.pallas import tpu as pltpu
from jax.sharding import PartitionSpec as P

F32 = jnp.float32
BF16 = jnp.bfloat16
EXPERTS = 16
CAP = 18
BODY = 16
REST = CAP - BODY
BLOCK = 40
CORES = 2
VMEM = 56 * 1024 * 1024


def dot(left, right):
    return lax.dot_general(left, right, (((1,), (0,)), ((), ())), preferred_element_type=F32)


def contract_rows(left, right):
    return lax.dot_general(left, right, (((0,), (0,)), ((), ())), preferred_element_type=F32)


def contract_last(left, right):
    return lax.dot_general(left, right, (((1,), (1,)), ((), ())), preferred_element_type=F32)


def named_and_earlier(routes):
    tokens = routes.shape[1]
    expert = lax.broadcasted_iota(jnp.int32, (EXPERTS, tokens), 0)
    first, second = expert == routes[0:1], expert == routes[1:2]
    earlier = lax.broadcasted_iota(jnp.int32, (tokens, tokens), 0) < lax.broadcasted_iota(
        jnp.int32, (tokens, tokens), 1
    )
    named = jnp.where(first | second, 1.0, 0.0).astype(BF16)
    count = dot(named, jnp.where(earlier, 1.0, 0.0).astype(BF16))
    return first, second, count.astype(jnp.int32)


def slots_of_rows(rows, lanes):
    row = lax.broadcasted_iota(jnp.int32, (1, rows, lanes), 1)
    one = jnp.where(row < BODY, row, -1)
    one = jnp.where((row >= 2 * BODY) & (row < 2 * BODY + REST), row - BODY, one)
    two = jnp.where((row >= BODY) & (row < 2 * BODY), row - BODY, -1)
    two = jnp.where((row >= 2 * BODY + REST) & (row < 2 * BODY + 2 * REST), row - BODY - REST, two)
    return one, two


def dispatch_kernel(routes, gates, tokens, cotangent, send, table, scale):
    @pl.when(pl.program_id(0) == 0)
    def _():
        first, second, count = named_and_earlier(routes[...])
        number = count.shape[1]
        held = jnp.where(first | second, count, -2)[:, None, :]
        one, two = slots_of_rows(BLOCK, number)
        gate = jnp.where(first, gates[0:1], 0.0) + jnp.where(second, gates[1:2], 0.0)
        in_one, in_two = held == one, held == two
        table[:, :number] = jnp.where(in_one, 1.0, 0.0).reshape(EXPERTS * BLOCK, number).astype(BF16)
        table[:, number:] = jnp.where(in_two, 1.0, 0.0).reshape(EXPERTS * BLOCK, number).astype(BF16)
        factor = jnp.where(in_two, gate[:, None, :], 0.0) + jnp.where(in_one, 1.0, 0.0)
        scale[...] = jnp.sum(factor.reshape(EXPERTS * BLOCK, number), axis=1, keepdims=True)

    both = jnp.concatenate([tokens[...], cotangent[...]], axis=0)
    rows = dot(table[...], both) * scale[...]
    send[...] = rows.astype(BF16).reshape(send.shape)


def dispatch(routes, gates, tokens, cotangent):
    number, width = tokens.shape
    step = 512
    whole = lambda i: (0, 0)
    column = lambda i: (0, i)
    return pl.pallas_call(
        dispatch_kernel,
        grid=(width // step,),
        in_specs=[
            pl.BlockSpec((2, number), whole),
            pl.BlockSpec((2, number), whole),
            pl.BlockSpec((number, step), column),
            pl.BlockSpec((number, step), column),
        ],
        out_specs=pl.BlockSpec((EXPERTS, BLOCK, step), lambda i: (0, 0, i)),
        out_shape=jax.ShapeDtypeStruct((EXPERTS, BLOCK, width), BF16),
        scratch_shapes=[
            pltpu.VMEM((EXPERTS * BLOCK, 2 * number), BF16),
            pltpu.VMEM((EXPERTS * BLOCK, 1), F32),
        ],
        compiler_params=pltpu.CompilerParams(vmem_limit_bytes=VMEM),
        name="dispatch",
    )(routes, gates, tokens, cotangent)


def expert_kernel(core, received, weights, act_out, dh_out, keep, give, part):
    width = received.shape[2]
    hidden = weights.shape[1] // 2
    body = EXPERTS * BODY
    x = received[:, :BODY, :].reshape(body, width)
    g = received[:, BODY : 2 * BODY, :].reshape(body, width)
    over = received[:, 2 * BODY :, :].reshape(EXPERTS * (BLOCK - 2 * BODY), width)
    rest = over.shape[0]
    up, down = weights[:, :hidden], weights[:, hidden:]
    valid = lax.broadcasted_iota(jnp.int32, (rest, hidden), 0) % (BLOCK - 2 * BODY) < REST

    def hidden_part(hpre, dact):
        s = 1.0 / (1.0 + jnp.exp(-hpre))
        return hpre * s, dact * s * (1.0 + hpre * (1.0 - s))

    act, dh = hidden_part(dot(x, up), dot(g, down))
    act, dh = act.astype(BF16), dh.astype(BF16)
    dact_over = pltpu.roll(dot(over, down), rest - REST, 0)
    act_over, dh_over = hidden_part(dot(over, up), dact_over)
    act_over = jnp.where(valid, act_over, 0.0)
    dh_over = jnp.where(valid, dh_over, 0.0).astype(BF16)
    act_moved = pltpu.roll(act_over, REST, 0).astype(BF16)
    act_out[:body] = act
    act_out[body:] = act_over.astype(BF16)
    dh_out[:body] = dh
    dh_out[body:] = dh_over
    part[:, :hidden] = (contract_rows(x, dh) + contract_rows(over, dh_over)).astype(BF16)
    part[:, hidden:] = (contract_rows(g, act) + contract_rows(over, act_moved)).astype(BF16)
    share = keep.shape[1]
    mine = core[0]
    for z in range(keep.shape[0]):
        at = z * CORES * share
        keep[z] = part[pl.ds(pl.multiple_of(at + mine * share, share), share), :]
        give[z] = part[pl.ds(pl.multiple_of(at + (1 - mine) * share, share), share), :]


def expert(core, received, weights, share):
    width = received.shape[2]
    wide = weights.shape[1]
    rows = EXPERTS * (BLOCK - BODY)
    whole = pl.BlockSpec(memory_space=pltpu.VMEM)
    chips = width // share // CORES
    return pl.pallas_call(
        expert_kernel,
        in_specs=[pl.BlockSpec(memory_space=pltpu.SMEM), whole, whole],
        out_specs=[whole] * 4,
        out_shape=[
            jax.ShapeDtypeStruct((rows, wide // 2), BF16),
            jax.ShapeDtypeStruct((rows, wide // 2), BF16),
            jax.ShapeDtypeStruct((chips, share, wide), BF16),
            jax.ShapeDtypeStruct((chips, share, wide), BF16),
        ],
        scratch_shapes=[pltpu.VMEM((width, wide), BF16)],
        compiler_params=pltpu.CompilerParams(vmem_limit_bytes=VMEM),
        name="expert",
    )(core, received, weights)


def return_kernel(act, dh, weights, back):
    hidden = weights.shape[1] // 2
    width = weights.shape[0]
    body = EXPERTS * BODY
    up, down = weights[:, :hidden], weights[:, hidden:]
    back[:, :BODY, :] = contract_last(act[:body], down).astype(BF16).reshape(EXPERTS, BODY, width)
    back[:, BODY : 2 * BODY, :] = (
        contract_last(dh[:body], up).astype(BF16).reshape(EXPERTS, BODY, width)
    )
    over = contract_last(act[body:], down) + pltpu.roll(contract_last(dh[body:], up), REST, 0)
    back[:, 2 * BODY :, :] = over.astype(BF16).reshape(EXPERTS, BLOCK - 2 * BODY, width)


def returns(act, dh, weights):
    whole = pl.BlockSpec(memory_space=pltpu.VMEM)
    return pl.pallas_call(
        return_kernel,
        in_specs=[whole] * 3,
        out_specs=whole,
        out_shape=jax.ShapeDtypeStruct((EXPERTS, BLOCK, weights.shape[0]), BF16),
        compiler_params=pltpu.CompilerParams(vmem_limit_bytes=VMEM),
        name="returns",
    )(act, dh, weights)


def combine_kernel(routes, gates, back, mixed, input_grad, table, scale):
    number = routes.shape[1]

    @pl.when(pl.program_id(0) == 0)
    def _():
        first, second, count = named_and_earlier(routes[...])
        one, two = slots_of_rows(BLOCK, number)

        def picked(chosen, slots):
            held = jnp.where(chosen, count, -2)[:, None, :]
            return jnp.where(held == slots, 1.0, 0.0).reshape(EXPERTS * BLOCK, number).astype(BF16)

        table[:, :number] = picked(first, one)
        table[:, number : 2 * number] = picked(second, one)
        table[:, 2 * number :] = picked(first | second, two)
        here = lax.broadcasted_iota(jnp.int32, (number, number), 0) == lax.broadcasted_iota(
            jnp.int32, (number, number), 1
        )
        for k in range(2):
            scale[k] = jnp.sum(jnp.where(here, gates[k : k + 1], 0.0), axis=1, keepdims=True)

    rows = back[...].reshape(EXPERTS * BLOCK, back.shape[2])
    pairs = contract_rows(table[...], rows)
    mixed[...] = (scale[0] * pairs[:number] + scale[1] * pairs[number : 2 * number]).astype(BF16)
    input_grad[...] = pairs[2 * number :].astype(BF16)


def combine(routes, gates, back):
    number = routes.shape[1]
    width = back.shape[2]
    step = 512
    whole = lambda i: (0, 0)
    column = pl.BlockSpec((number, step), lambda i: (0, i))
    return pl.pallas_call(
        combine_kernel,
        grid=(width // step,),
        in_specs=[
            pl.BlockSpec((2, number), whole),
            pl.BlockSpec((2, number), whole),
            pl.BlockSpec((EXPERTS, BLOCK, step), lambda i: (0, 0, i)),
        ],
        out_specs=[column, column],
        out_shape=[jax.ShapeDtypeStruct((number, width), BF16)] * 2,
        scratch_shapes=[
            pltpu.VMEM((EXPERTS * BLOCK, 3 * number), BF16),
            pltpu.VMEM((2, number, 1), F32),
        ],
        compiler_params=pltpu.CompilerParams(vmem_limit_bytes=VMEM),
        name="combine",
    )(routes, gates, back)


def local(chips, tokens, routes, gates, cotangent, up_weight, down_weight):
    hidden = up_weight.shape[2]
    share = up_weight.shape[1]
    at = lambda z, core: z * CORES + core
    across = [(at(z, c), at(z, 1 - c)) for z in range(chips) for c in range(CORES)]
    along_z = [[at(z, c) for z in range(chips)] for c in range(CORES)]
    weights = lax.all_gather(
        jnp.concatenate([up_weight[0], down_weight[0]], axis=1), "dp", axis=0, tiled=True
    )
    routes, gates = routes.T, gates.T
    send = dispatch(routes, gates, tokens, cotangent)
    received = lax.all_to_all(send, "expert", split_axis=0, concat_axis=0, tiled=True)
    core = (lax.axis_index("dp") % CORES).astype(jnp.int32).reshape(1)
    act, dh, keep, give = expert(core, received, weights, share)
    got = lax.ppermute(give, "dp", across)
    chip_sum = (keep.astype(F32) + got.astype(F32)).astype(BF16)
    summed = lax.psum_scatter(
        chip_sum, "dp", scatter_dimension=0, tiled=True, axis_index_groups=along_z
    )
    back = returns(act, dh, weights)
    back = lax.all_to_all(back, "expert", split_axis=0, concat_axis=0, tiled=True)
    mixed, input_grad = combine(routes, gates, back)
    return mixed, input_grad, summed[:, :, :hidden], summed[:, :, hidden:]


def solution(mesh):
    token = P(("dp", "expert"), None)
    weight = P("expert", "dp", None)
    return jax.shard_map(
        functools.partial(local, mesh.shape["dp"] // CORES),
        mesh=mesh,
        in_specs=(token, token, token, token, weight, weight),
        out_specs=(token, token, weight, weight),
        check_vma=False,
    )
```

```python
import functools

import jax
import jax.numpy as jnp
from jax import lax
from jax.experimental import pallas as pl
from jax.experimental.pallas import tpu as pltpu
from jax.sharding import PartitionSpec as P

F32 = jnp.float32
BF16 = jnp.bfloat16
EXPERTS = 16
CAP = 18
BODY = 16
REST = CAP - BODY
BLOCK = 40
CORES = 2
NOTE = 8
SMALL = 16 * 1024 * 1024
LARGE = 40 * 1024 * 1024
WHOLE = 60 * 1024 * 1024


def dot(left, right):
    return lax.dot_general(left, right, (((1,), (0,)), ((), ())), preferred_element_type=F32)


def contract_rows(left, right):
    return lax.dot_general(left, right, (((0,), (0,)), ((), ())), preferred_element_type=F32)


def contract_last(left, right):
    return lax.dot_general(left, right, (((1,), (1,)), ((), ())), preferred_element_type=F32)


def named_and_earlier(routes):
    tokens = routes.shape[1]
    expert = lax.broadcasted_iota(jnp.int32, (EXPERTS, tokens), 0)
    first, second = expert == routes[0:1], expert == routes[1:2]
    earlier = lax.broadcasted_iota(jnp.int32, (tokens, tokens), 0) < lax.broadcasted_iota(
        jnp.int32, (tokens, tokens), 1
    )
    named = jnp.where(first | second, 1.0, 0.0).astype(BF16)
    count = dot(named, jnp.where(earlier, 1.0, 0.0).astype(BF16))
    return first, second, count.astype(jnp.int32)


def slots_of_rows(rows, lanes):
    row = lax.broadcasted_iota(jnp.int32, (1, rows, lanes), 1)
    one = jnp.where(row < BODY, row, -1)
    one = jnp.where((row >= 2 * BODY) & (row < 2 * BODY + REST), row - BODY, one)
    two = jnp.where((row >= BODY) & (row < 2 * BODY), row - BODY, -1)
    two = jnp.where((row >= 2 * BODY + REST) & (row < 2 * BODY + 2 * REST), row - BODY - REST, two)
    return one, two


def coded(weight):
    rows = weight.astype(F32)
    peak = jnp.max(jnp.max(jnp.abs(rows), axis=1, keepdims=True), axis=0, keepdims=True)
    power = jnp.floor(jnp.log2(16384.0 / jnp.maximum(peak, 2.0**-100)))
    factor = jnp.exp2(power).astype(BF16).astype(F32)
    code = (rows * factor).astype(BF16)
    return jnp.concatenate([code, jnp.broadcast_to(power, (NOTE, rows.shape[1])).astype(BF16)], axis=0)


def dispatch_kernel(routes, gates, tokens, cotangent, up, down, send, codes, table, scale):
    @pl.when(pl.program_id(0) == 0)
    def _():
        hidden = up.shape[2]
        codes[:, :hidden] = coded(up[0])
        codes[:, hidden:] = coded(down[0])
        first, second, count = named_and_earlier(routes[...])
        number = count.shape[1]
        held = jnp.where(first | second, count, -2)[:, None, :]
        one, two = slots_of_rows(BLOCK, number)
        gate = jnp.where(first, gates[0:1], 0.0) + jnp.where(second, gates[1:2], 0.0)
        in_one, in_two = held == one, held == two
        table[:, :number] = jnp.where(in_one, 1.0, 0.0).reshape(EXPERTS * BLOCK, number).astype(BF16)
        table[:, number:] = jnp.where(in_two, 1.0, 0.0).reshape(EXPERTS * BLOCK, number).astype(BF16)
        factor = jnp.where(in_two, gate[:, None, :], 0.0) + jnp.where(in_one, 1.0, 0.0)
        scale[...] = jnp.sum(factor.reshape(EXPERTS * BLOCK, number), axis=1, keepdims=True)

    both = jnp.concatenate([tokens[...], cotangent[...]], axis=0)
    rows = dot(table[...], both) * scale[...]
    send[...] = rows.astype(BF16).reshape(send.shape)


def dispatch(routes, gates, tokens, cotangent, up_weight, down_weight):
    number, width = tokens.shape
    share, hidden = up_weight.shape[1:]
    step = 512
    whole = lambda i: (0, 0)
    column = lambda i: (0, i)
    return pl.pallas_call(
        dispatch_kernel,
        grid=(width // step,),
        in_specs=[
            pl.BlockSpec((2, number), whole),
            pl.BlockSpec((2, number), whole),
            pl.BlockSpec((number, step), column),
            pl.BlockSpec((number, step), column),
            pl.BlockSpec((1, share, hidden), lambda i: (0, 0, 0)),
            pl.BlockSpec((1, share, hidden), lambda i: (0, 0, 0)),
        ],
        out_specs=[
            pl.BlockSpec((EXPERTS, BLOCK, step), lambda i: (0, 0, i)),
            pl.BlockSpec((share + NOTE, 2 * hidden), whole),
        ],
        out_shape=[
            jax.ShapeDtypeStruct((EXPERTS, BLOCK, width), BF16),
            jax.ShapeDtypeStruct((share + NOTE, 2 * hidden), BF16),
        ],
        scratch_shapes=[
            pltpu.VMEM((EXPERTS * BLOCK, 2 * number), BF16),
            pltpu.VMEM((EXPERTS * BLOCK, 1), F32),
        ],
        compiler_params=pltpu.CompilerParams(vmem_limit_bytes=WHOLE),
        name="dispatch",
    )(routes, gates, tokens, cotangent, up_weight, down_weight)


def offset_of(r, core):
    return (0, 1, 2 - 4 * core, -1)[r]


def expert_kernel(place, received, codes, act_out, dh_out, weights, keep, give, part):
    width = received.shape[2]
    hidden = codes.shape[2] // 2
    rows = codes.shape[1] - NOTE
    factor = jnp.exp2(-codes[:, rows:, :].astype(F32)).astype(BF16)[:, :1, :]
    weights[...] = (codes[:, :rows, :] * factor).reshape(weights.shape)
    body = EXPERTS * BODY
    x = received[:, :BODY, :].reshape(body, width)
    g = received[:, BODY : 2 * BODY, :].reshape(body, width)
    over = received[:, 2 * BODY :, :].reshape(EXPERTS * (BLOCK - 2 * BODY), width)
    rest = over.shape[0]
    up, down = weights[:, :hidden], weights[:, hidden:]
    valid = lax.broadcasted_iota(jnp.int32, (rest, hidden), 0) % (BLOCK - 2 * BODY) < REST

    def hidden_part(hpre, dact):
        s = 1.0 / (1.0 + jnp.exp(-hpre))
        return hpre * s, dact * s * (1.0 + hpre * (1.0 - s))

    act, dh = hidden_part(dot(x, up), dot(g, down))
    act, dh = act.astype(BF16), dh.astype(BF16)
    dact_over = pltpu.roll(dot(over, down), rest - REST, 0)
    act_over, dh_over = hidden_part(dot(over, up), dact_over)
    act_over = jnp.where(valid, act_over, 0.0)
    dh_over = jnp.where(valid, dh_over, 0.0).astype(BF16)
    act_moved = pltpu.roll(act_over, REST, 0).astype(BF16)
    act_out[:body] = act
    act_out[body:] = act_over.astype(BF16)
    dh_out[:body] = dh
    dh_out[body:] = dh_over
    part[:, :hidden] = (contract_rows(x, dh) + contract_rows(over, dh_over)).astype(BF16)
    part[:, hidden:] = (contract_rows(g, act) + contract_rows(over, act_moved)).astype(BF16)
    near, far, share = keep.shape[:3]
    z, mine = place[0], place[1]
    for out, owner in ((keep, mine), (give, 1 - mine)):
        for r in range(near):
            for j in range(far):
                chip = lax.rem(z + offset_of(r, owner) + near * j + near * far, near * far)
                at = (chip * CORES + owner) * share
                out[r, j] = part[pl.ds(pl.multiple_of(at, share), share), :]


def expert(place, received, codes):
    width = received.shape[2]
    wide = codes.shape[2]
    share = codes.shape[1] - NOTE
    rows = EXPERTS * (BLOCK - BODY)
    whole = pl.BlockSpec(memory_space=pltpu.VMEM)
    near = 4
    far = width // share // CORES // near
    return pl.pallas_call(
        expert_kernel,
        in_specs=[pl.BlockSpec(memory_space=pltpu.SMEM), whole, whole],
        out_specs=[whole] * 5,
        out_shape=[
            jax.ShapeDtypeStruct((rows, wide // 2), BF16),
            jax.ShapeDtypeStruct((rows, wide // 2), BF16),
            jax.ShapeDtypeStruct((width, wide), BF16),
            jax.ShapeDtypeStruct((near, far, share, wide), BF16),
            jax.ShapeDtypeStruct((near, far, share, wide), BF16),
        ],
        scratch_shapes=[pltpu.VMEM((width, wide), BF16)],
        compiler_params=pltpu.CompilerParams(vmem_limit_bytes=LARGE),
        name="expert",
    )(place, received, codes)


def return_kernel(act, dh, weights, back):
    hidden = weights.shape[1] // 2
    width = weights.shape[0]
    body = EXPERTS * BODY
    up, down = weights[:, :hidden], weights[:, hidden:]
    back[:, :BODY, :] = contract_last(act[:body], down).astype(BF16).reshape(EXPERTS, BODY, width)
    back[:, BODY : 2 * BODY, :] = (
        contract_last(dh[:body], up).astype(BF16).reshape(EXPERTS, BODY, width)
    )
    over = contract_last(act[body:], down) + pltpu.roll(contract_last(dh[body:], up), REST, 0)
    back[:, 2 * BODY :, :] = over.astype(BF16).reshape(EXPERTS, BLOCK - 2 * BODY, width)


def returns(act, dh, weights):
    whole = pl.BlockSpec(memory_space=pltpu.VMEM)
    return pl.pallas_call(
        return_kernel,
        in_specs=[whole] * 3,
        out_specs=whole,
        out_shape=jax.ShapeDtypeStruct((EXPERTS, BLOCK, weights.shape[0]), BF16),
        compiler_params=pltpu.CompilerParams(vmem_limit_bytes=LARGE),
        name="returns",
    )(act, dh, weights)


def table_kernel(routes, gates, table, scale):
    number = routes.shape[1]
    first, second, count = named_and_earlier(routes[...])
    one, two = slots_of_rows(BLOCK, number)

    def picked(chosen, slots):
        held = jnp.where(chosen, count, -2)[:, None, :]
        return jnp.where(held == slots, 1.0, 0.0).reshape(EXPERTS * BLOCK, number).T.astype(BF16)

    table[:number] = picked(first, one)
    table[number : 2 * number] = picked(second, one)
    table[2 * number :] = picked(first | second, two)
    here = lax.broadcasted_iota(jnp.int32, (number, number), 0) == lax.broadcasted_iota(
        jnp.int32, (number, number), 1
    )
    for k in range(2):
        scale[k] = jnp.sum(jnp.where(here, gates[k : k + 1], 0.0), axis=1, keepdims=True)


def tables(routes, gates):
    number = routes.shape[1]
    return pl.pallas_call(
        table_kernel,
        out_shape=[
            jax.ShapeDtypeStruct((3 * number, EXPERTS * BLOCK), BF16),
            jax.ShapeDtypeStruct((2, number, 1), F32),
        ],
        compiler_params=pltpu.CompilerParams(vmem_limit_bytes=SMALL),
        name="tables",
    )(routes, gates)


def combine_kernel(table, scale, back, mixed, input_grad):
    number = mixed.shape[0]
    rows = back[...].reshape(EXPERTS * BLOCK, back.shape[2])
    pairs = dot(table[...], rows)
    mixed[...] = (scale[0] * pairs[:number] + scale[1] * pairs[number : 2 * number]).astype(BF16)
    input_grad[...] = pairs[2 * number :].astype(BF16)


def combine(table, scale, back):
    number = scale.shape[1]
    width = back.shape[2]
    step = 512
    column = pl.BlockSpec((number, step), lambda i: (0, i))
    return pl.pallas_call(
        combine_kernel,
        grid=(width // step,),
        in_specs=[
            pl.BlockSpec(table.shape, lambda i: (0, 0)),
            pl.BlockSpec(scale.shape, lambda i: (0, 0, 0)),
            pl.BlockSpec((EXPERTS, BLOCK, step), lambda i: (0, 0, i)),
        ],
        out_specs=[column, column],
        out_shape=[jax.ShapeDtypeStruct((number, width), BF16)] * 2,
        compiler_params=pltpu.CompilerParams(vmem_limit_bytes=SMALL),
        name="combine",
    )(table, scale, back)


def local(chips, tokens, routes, gates, cotangent, up_weight, down_weight):
    hidden = up_weight.shape[2]
    near = 4
    far = chips // near

    def moved(array, hops):
        pairs = []
        for z in range(chips):
            for core in range(CORES):
                to = z * CORES + 1 - core if hops is None else (z + hops(core)) % chips * CORES + core
                pairs.append((z * CORES + core, to))
        return lax.ppermute(array, "dp", pairs)

    routes, gates = routes.T, gates.T
    send, codes = dispatch(routes, gates, tokens, cotangent, up_weight, down_weight)
    codes = lax.all_gather(codes.astype(jnp.float16), "dp").astype(BF16)
    received = lax.all_to_all(send, "expert", split_axis=0, concat_axis=0, tiled=True)
    me = lax.axis_index("dp").astype(jnp.int32)
    place = jnp.stack([me // CORES, me % CORES])
    act, dh, weights, keep, give = expert(place, received, codes)
    got = moved(give, None)

    def total(*arrays):
        return sum(a.astype(F32) for a in arrays)

    quarter = total(keep[0], got[0])
    for r in range(1, near):
        chip_sum = total(keep[r], got[r]).astype(BF16)
        arrived = moved(chip_sum, lambda core: offset_of(r, core))
        quarter = quarter + arrived.astype(F32)
    quarter = quarter.astype(BF16)
    arrived = [moved(quarter[j], lambda core: near * j) for j in range(1, far)]
    table, scale = tables(routes, gates)
    back = returns(act, dh, weights)
    back = lax.all_to_all(back, "expert", split_axis=0, concat_axis=0, tiled=True)
    mixed, input_grad = combine(table, scale, back)
    mixed, input_grad, arrived = lax.optimization_barrier((mixed, input_grad, arrived))
    summed = total(quarter[0], *arrived).astype(BF16)[None]
    return mixed, input_grad, summed[:, :, :hidden], summed[:, :, hidden:]


def solution(mesh):
    token = P(("dp", "expert"), None)
    weight = P("expert", "dp", None)
    return jax.shard_map(
        functools.partial(local, mesh.shape["dp"] // CORES),
        mesh=mesh,
        in_specs=(token, token, token, token, weight, weight),
        out_specs=(token, token, weight, weight),
        check_vma=False,
    )
```

```python
import functools

import jax
import jax.numpy as jnp
from jax import lax
from jax.experimental import pallas as pl
from jax.experimental.pallas import tpu as pltpu
from jax.sharding import PartitionSpec as P

F32 = jnp.float32
BF16 = jnp.bfloat16
EXPERTS = 16
CAP = 18
BODY = 16
REST = CAP - BODY
BLOCK = 40
CORES = 2
NOTE = 8
SMALL = 16 * 1024 * 1024
LARGE = 40 * 1024 * 1024
WHOLE = 60 * 1024 * 1024
LONG = pl.CostEstimate(flops=50_000_000_000, bytes_accessed=1_000_000, transcendentals=0)


def dot(left, right):
    return lax.dot_general(left, right, (((1,), (0,)), ((), ())), preferred_element_type=F32)


def contract_rows(left, right):
    return lax.dot_general(left, right, (((0,), (0,)), ((), ())), preferred_element_type=F32)


def contract_last(left, right):
    return lax.dot_general(left, right, (((1,), (1,)), ((), ())), preferred_element_type=F32)


def named_and_earlier(routes):
    tokens = routes.shape[1]
    expert = lax.broadcasted_iota(jnp.int32, (EXPERTS, tokens), 0)
    first, second = expert == routes[0:1], expert == routes[1:2]
    earlier = lax.broadcasted_iota(jnp.int32, (tokens, tokens), 0) < lax.broadcasted_iota(
        jnp.int32, (tokens, tokens), 1
    )
    named = jnp.where(first | second, 1.0, 0.0).astype(BF16)
    count = dot(named, jnp.where(earlier, 1.0, 0.0).astype(BF16))
    return first, second, count.astype(jnp.int32)


def slots_of_rows(rows, lanes):
    row = lax.broadcasted_iota(jnp.int32, (1, rows, lanes), 1)
    one = jnp.where(row < BODY, row, -1)
    one = jnp.where((row >= 2 * BODY) & (row < 2 * BODY + REST), row - BODY, one)
    two = jnp.where((row >= BODY) & (row < 2 * BODY), row - BODY, -1)
    two = jnp.where((row >= 2 * BODY + REST) & (row < 2 * BODY + 2 * REST), row - BODY - REST, two)
    return one, two


def coded(weight):
    rows = weight.astype(F32)
    peak = jnp.max(jnp.max(jnp.abs(rows), axis=1, keepdims=True), axis=0, keepdims=True)
    power = jnp.floor(jnp.log2(16384.0 / jnp.maximum(peak, 2.0**-100)))
    factor = jnp.exp2(power).astype(BF16).astype(F32)
    code = (rows * factor).astype(BF16)
    return jnp.concatenate([code, jnp.broadcast_to(power, (NOTE, rows.shape[1])).astype(BF16)], axis=0)


def dispatch_kernel(
    routes, gates, up, down, tokens, cotangent, send, codes, both, table, rows, in_sems, out_sems
):
    number, width = tokens.shape
    step = rows.shape[3]
    loads = [
        pltpu.make_async_copy(source, both.at[pl.ds(k * number, number)], in_sems.at[k])
        for k, source in enumerate((tokens, cotangent))
    ]
    for load in loads:
        load.start()
    hidden = up.shape[2]
    codes[:, :hidden] = coded(up[0])
    codes[:, hidden:] = coded(down[0])
    first, second, count = named_and_earlier(routes[...])
    held = jnp.where(first | second, count, -2)[:, None, :]
    one, two = slots_of_rows(BLOCK, number)
    gate = jnp.where(first, gates[0:1], 0.0) + jnp.where(second, gates[1:2], 0.0)
    in_one, in_two = held == one, held == two
    table[:, :number] = jnp.where(in_one, 1.0, 0.0).reshape(EXPERTS * BLOCK, number).astype(BF16)
    table[:, number:] = jnp.where(in_two, 1.0, 0.0).reshape(EXPERTS * BLOCK, number).astype(BF16)
    scale = jnp.where(in_two, gate[:, None, :], 0.0) + jnp.where(in_one, 1.0, 0.0)
    scale = jnp.sum(scale.reshape(EXPERTS * BLOCK, number), axis=1, keepdims=True)
    for load in loads:
        load.wait()
    stores = []
    for k in range(width // step):
        columns = pl.ds(k * step, step)
        block = dot(table[...], both[:, columns]) * scale
        rows[k] = block.astype(BF16).reshape(EXPERTS, BLOCK, step)
        stores.append(pltpu.make_async_copy(rows.at[k], send.at[:, :, columns], out_sems.at[k]))
        stores[-1].start()
    for store in stores:
        store.wait()


def dispatch(routes, gates, tokens, cotangent, up_weight, down_weight):
    number, width = tokens.shape
    share, hidden = up_weight.shape[1:]
    step = 512
    steps = width // step
    vmem = pl.BlockSpec(memory_space=pltpu.VMEM)
    anywhere = pl.BlockSpec(memory_space=pl.ANY)
    return pl.pallas_call(
        dispatch_kernel,
        in_specs=[vmem] * 4 + [anywhere] * 2,
        out_specs=[anywhere, vmem],
        out_shape=[
            jax.ShapeDtypeStruct((EXPERTS, BLOCK, width), BF16),
            jax.ShapeDtypeStruct((share + NOTE, 2 * hidden), BF16),
        ],
        scratch_shapes=[
            pltpu.VMEM((2 * number, width), BF16),
            pltpu.VMEM((EXPERTS * BLOCK, 2 * number), BF16),
            pltpu.VMEM((steps, EXPERTS, BLOCK, step), BF16),
            pltpu.SemaphoreType.DMA((2,)),
            pltpu.SemaphoreType.DMA((steps,)),
        ],
        compiler_params=pltpu.CompilerParams(vmem_limit_bytes=WHOLE),
        name="dispatch",
    )(routes, gates, up_weight, down_weight, tokens, cotangent)


def offset_of(r, core):
    return (0, 1, 2 - 4 * core, -1)[r]


def expert_kernel(place, received, codes, act_out, dh_out, weights, keep, give, part):
    width = received.shape[2]
    hidden = codes.shape[2] // 2
    rows = codes.shape[1] - NOTE
    factor = jnp.exp2(-codes[:, rows:, :].astype(F32)).astype(BF16)[:, :1, :]
    weights[...] = (codes[:, :rows, :] * factor).reshape(weights.shape)
    body = EXPERTS * BODY
    x = received[:, :BODY, :].reshape(body, width)
    g = received[:, BODY : 2 * BODY, :].reshape(body, width)
    over = received[:, 2 * BODY :, :].reshape(EXPERTS * (BLOCK - 2 * BODY), width)
    rest = over.shape[0]
    up, down = weights[:, :hidden], weights[:, hidden:]
    valid = lax.broadcasted_iota(jnp.int32, (rest, hidden), 0) % (BLOCK - 2 * BODY) < REST

    def hidden_part(hpre, dact):
        s = 1.0 / (1.0 + jnp.exp(-hpre))
        return hpre * s, dact * s * (1.0 + hpre * (1.0 - s))

    act, dh = hidden_part(dot(x, up), dot(g, down))
    act, dh = act.astype(BF16), dh.astype(BF16)
    dact_over = pltpu.roll(dot(over, down), rest - REST, 0)
    act_over, dh_over = hidden_part(dot(over, up), dact_over)
    act_over = jnp.where(valid, act_over, 0.0)
    dh_over = jnp.where(valid, dh_over, 0.0).astype(BF16)
    act_moved = pltpu.roll(act_over, REST, 0).astype(BF16)
    act_out[:body] = act
    act_out[body:] = act_over.astype(BF16)
    dh_out[:body] = dh
    dh_out[body:] = dh_over
    part[:, :hidden] = (contract_rows(x, dh) + contract_rows(over, dh_over)).astype(BF16)
    part[:, hidden:] = (contract_rows(g, act) + contract_rows(over, act_moved)).astype(BF16)
    near, far, share = keep.shape[:3]
    z, mine = place[0], place[1]
    for out, owner in ((keep, mine), (give, 1 - mine)):
        for r in range(near):
            for j in range(far):
                chip = lax.rem(z + offset_of(r, owner) + near * j + near * far, near * far)
                at = (chip * CORES + owner) * share
                out[r, j] = part[pl.ds(pl.multiple_of(at, share), share), :]


def expert(place, received, codes):
    width = received.shape[2]
    wide = codes.shape[2]
    share = codes.shape[1] - NOTE
    rows = EXPERTS * (BLOCK - BODY)
    whole = pl.BlockSpec(memory_space=pltpu.VMEM)
    near = 4
    far = width // share // CORES // near
    return pl.pallas_call(
        expert_kernel,
        in_specs=[pl.BlockSpec(memory_space=pltpu.SMEM), whole, whole],
        out_specs=[whole] * 5,
        out_shape=[
            jax.ShapeDtypeStruct((rows, wide // 2), BF16),
            jax.ShapeDtypeStruct((rows, wide // 2), BF16),
            jax.ShapeDtypeStruct((width, wide), BF16),
            jax.ShapeDtypeStruct((near, far, share, wide), BF16),
            jax.ShapeDtypeStruct((near, far, share, wide), BF16),
        ],
        scratch_shapes=[pltpu.VMEM((width, wide), BF16)],
        compiler_params=pltpu.CompilerParams(vmem_limit_bytes=LARGE),
        name="expert",
    )(place, received, codes)


def return_kernel(act, dh, weights, back):
    hidden = weights.shape[1] // 2
    half = weights.shape[0] // 2
    body = EXPERTS * BODY
    over = jnp.zeros((act.shape[0] - body, half), F32)
    for kind, value in enumerate((act, dh)):
        for side in range(2):
            place = 2 * kind + side
            weight = weights[side * half : (side + 1) * half, (1 - kind) * hidden : (2 - kind) * hidden]
            back[:, place * BODY : (place + 1) * BODY, :] = (
                contract_last(value[:body], weight).astype(BF16).reshape(EXPERTS, BODY, half)
            )
            rest = contract_last(value[body:], weight)
            over = over + (pltpu.roll(rest, REST * place, 0) if place else rest)
    back[:, 4 * BODY :, :] = over.astype(BF16).reshape(EXPERTS, 4 * REST, half)


def returns(act, dh, weights):
    whole = pl.BlockSpec(memory_space=pltpu.VMEM)
    return pl.pallas_call(
        return_kernel,
        in_specs=[whole] * 3,
        out_specs=whole,
        out_shape=jax.ShapeDtypeStruct((EXPERTS, 4 * CAP, weights.shape[0] // 2), BF16),
        compiler_params=pltpu.CompilerParams(vmem_limit_bytes=LARGE),
        cost_estimate=LONG,
        name="returns",
    )(act, dh, weights)


def table_kernel(routes, gates, table, scale):
    number = routes.shape[1]
    first, second, count = named_and_earlier(routes[...])
    slot = lax.broadcasted_iota(jnp.int32, (1, BODY, number), 1)
    place = lax.broadcasted_iota(jnp.int32, (1, 4 * REST, number), 1)
    for k, chosen in enumerate((first, second, first | second)):
        held = jnp.where(chosen, count, -2)[:, None, :]
        body = jnp.where(held == slot, 1.0, 0.0).reshape(EXPERTS * BODY, number).T
        for side in range(2):
            start = REST * (2 * (k // 2) + side)
            mine = (place >= start) & (place < start + REST)
            over = jnp.where(mine & (held == place - start + BODY), 1.0, 0.0)
            over = over.reshape(EXPERTS * 4 * REST, number).T
            at = slice(k * number, (k + 1) * number)
            table[side, at] = jnp.concatenate([body, over], axis=1).astype(BF16)
    here = lax.broadcasted_iota(jnp.int32, (number, number), 0) == lax.broadcasted_iota(
        jnp.int32, (number, number), 1
    )
    for k in range(2):
        scale[k] = jnp.sum(jnp.where(here, gates[k : k + 1], 0.0), axis=1, keepdims=True)


def tables(routes, gates):
    number = routes.shape[1]
    return pl.pallas_call(
        table_kernel,
        out_shape=[
            jax.ShapeDtypeStruct((2, 3 * number, EXPERTS * (BODY + 4 * REST)), BF16),
            jax.ShapeDtypeStruct((2, number, 1), F32),
        ],
        compiler_params=pltpu.CompilerParams(vmem_limit_bytes=SMALL),
        cost_estimate=LONG,
        name="tables",
    )(routes, gates)


def combine_kernel(table, scale, back, mixed, input_grad):
    number = mixed.shape[0]
    half = back.shape[2]
    over = back[:, 4 * BODY :, :].reshape(EXPERTS * 4 * REST, half)
    for side in range(2):
        columns = slice(side * half, (side + 1) * half)
        kinds = []
        for kind in range(2):
            at = (2 * kind + side) * BODY
            body = back[:, at : at + BODY, :].reshape(EXPERTS * BODY, half)
            kinds.append(jnp.concatenate([body, over], axis=0))
        pairs = dot(table[side, : 2 * number], kinds[0])
        mixed[:, columns] = (scale[0] * pairs[:number] + scale[1] * pairs[number:]).astype(BF16)
        input_grad[:, columns] = dot(table[side, 2 * number :], kinds[1]).astype(BF16)


def combine(table, scale, back):
    number = scale.shape[1]
    width = 2 * back.shape[2]
    return pl.pallas_call(
        combine_kernel,
        out_shape=[jax.ShapeDtypeStruct((number, width), BF16)] * 2,
        compiler_params=pltpu.CompilerParams(vmem_limit_bytes=SMALL),
        name="combine",
    )(table, scale, back)


def last_kernel(own, first, second, third, up, down):
    hidden = up.shape[2]
    summed = own[...].astype(F32) + first[...].astype(F32)
    summed = summed + second[...].astype(F32) + third[...].astype(F32)
    up[0] = summed[:, :hidden].astype(BF16)
    down[0] = summed[:, hidden:].astype(BF16)


def last_sum(own, arrived):
    share, wide = own.shape
    grad = jax.ShapeDtypeStruct((1, share, wide // 2), BF16)
    return pl.pallas_call(last_kernel, out_shape=[grad, grad], name="last_sum")(own, *arrived)


def local(chips, tokens, routes, gates, cotangent, up_weight, down_weight):
    near = 4
    far = chips // near

    def moved(array, hops):
        pairs = []
        for z in range(chips):
            for core in range(CORES):
                to = z * CORES + 1 - core if hops is None else (z + hops(core)) % chips * CORES + core
                pairs.append((z * CORES + core, to))
        return lax.ppermute(array, "dp", pairs)

    routes, gates = routes.T, gates.T
    send, codes = dispatch(routes, gates, tokens, cotangent, up_weight, down_weight)
    codes = lax.all_gather(codes.astype(jnp.float16), "dp").astype(BF16)
    received = lax.all_to_all(send, "expert", split_axis=0, concat_axis=0, tiled=True)
    me = lax.axis_index("dp").astype(jnp.int32)
    place = jnp.stack([me // CORES, me % CORES])
    act, dh, weights, keep, give = expert(place, received, codes)
    got = moved(give, None)

    def total(*arrays):
        return sum(a.astype(F32) for a in arrays)

    got, back = lax.optimization_barrier((got, returns(act, dh, weights)))
    quarter = total(keep[0], got[0])
    for r in range(1, near):
        chip_sum = total(keep[r], got[r]).astype(BF16)
        arrived = moved(chip_sum, lambda core: offset_of(r, core))
        quarter = quarter + arrived.astype(F32)
    quarter = quarter.astype(BF16)
    arrived = [moved(quarter[j], lambda core: near * j) for j in range(1, far)]
    routes, gates, quarter = lax.optimization_barrier((routes, gates, quarter))
    table, scale = tables(routes, gates)
    back = lax.all_to_all(back, "expert", split_axis=0, concat_axis=0, tiled=True)
    mixed, input_grad = combine(table, scale, back)
    mixed, input_grad, arrived = lax.optimization_barrier((mixed, input_grad, arrived))
    up_grad, down_grad = last_sum(quarter[0], arrived)
    return mixed, input_grad, up_grad, down_grad


def solution(mesh):
    token = P(("dp", "expert"), None)
    weight = P("expert", "dp", None)
    return jax.shard_map(
        functools.partial(local, mesh.shape["dp"] // CORES),
        mesh=mesh,
        in_specs=(token, token, token, token, weight, weight),
        out_specs=(token, token, weight, weight),
        check_vma=False,
    )
```

```python
import functools

import jax
import jax.numpy as jnp
from jax import lax
from jax.experimental import pallas as pl
from jax.experimental.pallas import tpu as pltpu
from jax.sharding import PartitionSpec as P

F32 = jnp.float32
BF16 = jnp.bfloat16
EXPERTS = 16
CAP = 18
BODY = 16
REST = CAP - BODY
BLOCK = 40
CORES = 2
NOTE = 8
SMALL = 16 * 1024 * 1024
LARGE = 40 * 1024 * 1024
WHOLE = 60 * 1024 * 1024
LONG = pl.CostEstimate(flops=50_000_000_000, bytes_accessed=1_000_000, transcendentals=0)


def dot(left, right):
    return lax.dot_general(left, right, (((1,), (0,)), ((), ())), preferred_element_type=F32)


def contract_rows(left, right):
    return lax.dot_general(left, right, (((0,), (0,)), ((), ())), preferred_element_type=F32)


def contract_last(left, right):
    return lax.dot_general(left, right, (((1,), (1,)), ((), ())), preferred_element_type=F32)


def named_and_earlier(routes):
    tokens = routes.shape[1]
    expert = lax.broadcasted_iota(jnp.int32, (EXPERTS, tokens), 0)
    first, second = expert == routes[0:1], expert == routes[1:2]
    earlier = lax.broadcasted_iota(jnp.int32, (tokens, tokens), 0) < lax.broadcasted_iota(
        jnp.int32, (tokens, tokens), 1
    )
    named = jnp.where(first | second, 1.0, 0.0).astype(BF16)
    count = dot(named, jnp.where(earlier, 1.0, 0.0).astype(BF16))
    return first, second, count.astype(jnp.int32)


def slots_of_rows(rows, lanes):
    row = lax.broadcasted_iota(jnp.int32, (1, rows, lanes), 1)
    one = jnp.where(row < BODY, row, -1)
    one = jnp.where((row >= 2 * BODY) & (row < 2 * BODY + REST), row - BODY, one)
    two = jnp.where((row >= BODY) & (row < 2 * BODY), row - BODY, -1)
    two = jnp.where((row >= 2 * BODY + REST) & (row < 2 * BODY + 2 * REST), row - BODY - REST, two)
    return one, two


def coded(weight):
    rows = weight.astype(F32)
    peak = jnp.max(jnp.max(jnp.abs(rows), axis=1, keepdims=True), axis=0, keepdims=True)
    power = jnp.floor(jnp.log2(16384.0 / jnp.maximum(peak, 2.0**-100)))
    factor = jnp.exp2(power).astype(BF16).astype(F32)
    code = (rows * factor).astype(BF16)
    return jnp.concatenate([code, jnp.broadcast_to(power, (NOTE, rows.shape[1])).astype(BF16)], axis=0)


def dispatch_kernel(
    routes, gates, up, down, tokens, cotangent, send, codes,
    routes_in, gates_in, up_in, down_in, both, table, rows, small_sems, in_sems, out_sems,
):
    number, width = tokens.shape
    steps, step = rows.shape[:2]
    small = [
        pltpu.make_async_copy(source, target, small_sems.at[k])
        for k, (source, target) in enumerate(
            ((routes, routes_in), (gates, gates_in), (up, up_in), (down, down_in))
        )
    ]
    large = [
        pltpu.make_async_copy(source, both.at[pl.ds(k * number, number)], in_sems.at[k])
        for k, source in enumerate((tokens, cotangent))
    ]
    for load in small + large:
        load.start()
    for load in small:
        load.wait()
    hidden = up.shape[2]
    codes[:, :hidden] = coded(up_in[0])
    codes[:, hidden:] = coded(down_in[0])
    first, second, count = named_and_earlier(routes_in[...])
    held = jnp.where(first | second, count, -2)[:, None, :]
    one, two = slots_of_rows(BLOCK, number)
    gate = jnp.where(first, gates_in[0:1], 0.0) + jnp.where(second, gates_in[1:2], 0.0)
    in_one, in_two = held == one, held == two
    table[:, :number] = jnp.where(in_one, 1.0, 0.0).reshape(EXPERTS * BLOCK, number).astype(BF16)
    table[:, number:] = jnp.where(in_two, 1.0, 0.0).reshape(EXPERTS * BLOCK, number).astype(BF16)
    scale = jnp.where(in_two, gate[:, None, :], 0.0) + jnp.where(in_one, 1.0, 0.0)
    scale = jnp.sum(scale.reshape(EXPERTS * BLOCK, number), axis=1, keepdims=True)
    for load in large:
        load.wait()
    stores = []
    for k in range(steps):
        at = slice(k * step * BLOCK, (k + 1) * step * BLOCK)
        block = dot(table[at], both[...]) * scale[at]
        rows[k] = block.astype(BF16).reshape(step, BLOCK, width)
        stores.append(
            pltpu.make_async_copy(rows.at[k], send.at[pl.ds(k * step, step)], out_sems.at[k])
        )
        stores[-1].start()
    for store in stores:
        store.wait()


def dispatch(routes, gates, tokens, cotangent, up_weight, down_weight):
    number, width = tokens.shape
    share, hidden = up_weight.shape[1:]
    step = 4
    steps = EXPERTS // step
    anywhere = pl.BlockSpec(memory_space=pl.ANY)
    return pl.pallas_call(
        dispatch_kernel,
        in_specs=[anywhere] * 6,
        out_specs=[anywhere, pl.BlockSpec(memory_space=pltpu.VMEM)],
        out_shape=[
            jax.ShapeDtypeStruct((EXPERTS, BLOCK, width), BF16),
            jax.ShapeDtypeStruct((share + NOTE, 2 * hidden), BF16),
        ],
        scratch_shapes=[
            pltpu.VMEM(routes.shape, jnp.int32),
            pltpu.VMEM(gates.shape, F32),
            pltpu.VMEM(up_weight.shape, BF16),
            pltpu.VMEM(down_weight.shape, BF16),
            pltpu.VMEM((2 * number, width), BF16),
            pltpu.VMEM((EXPERTS * BLOCK, 2 * number), BF16),
            pltpu.VMEM((steps, step, BLOCK, width), BF16),
            pltpu.SemaphoreType.DMA((4,)),
            pltpu.SemaphoreType.DMA((2,)),
            pltpu.SemaphoreType.DMA((steps,)),
        ],
        compiler_params=pltpu.CompilerParams(vmem_limit_bytes=WHOLE),
        name="dispatch",
    )(routes, gates, up_weight, down_weight, tokens, cotangent)


def offset_of(r, core):
    return (0, 1, 2 - 4 * core, -1)[r]


def ones_where(rows, columns, chosen):
    row = lax.broadcasted_iota(jnp.int32, (rows, columns), 0)
    column = lax.broadcasted_iota(jnp.int32, (rows, columns), 1)
    return jnp.where(chosen(row) == column, 1.0, 0.0).astype(BF16)


def expert_kernel(
    place, received, codes, act_out, dh_out, weights, keep, give, x, g
):
    width = received.shape[2]
    hidden = codes.shape[2] // 2
    share = codes.shape[1] - NOTE
    body = EXPERTS * BODY
    rest = EXPERTS * REST
    factor = jnp.exp2(-codes[:, share:, :].astype(F32)).astype(BF16)[:, :1, :]
    weights[...] = (codes[:, :share, :] * factor).reshape(weights.shape)
    x[:body] = received[:, :BODY, :].reshape(body, width)
    g[:body] = received[:, BODY : 2 * BODY, :].reshape(body, width)
    eight = BLOCK - 2 * BODY
    over = received[:, 2 * BODY :, :].reshape(EXPERTS * eight, width)
    pick = ones_where(
        2 * rest,
        EXPERTS * eight,
        lambda row: (row % rest) // REST * eight + row // rest * REST + row % REST,
    )
    over = dot(pick, over).astype(BF16)
    x[body:] = over[:rest]
    g[body:] = over[rest:]
    hpre = dot(x[...], weights[:, :hidden])
    dact = dot(g[...], weights[:, hidden:])
    s = 1.0 / (1.0 + jnp.exp(-hpre))
    act = (hpre * s).astype(BF16)
    dh = (dact * s * (1.0 + hpre * (1.0 - s))).astype(BF16)
    act_out[...] = act
    dh_out[...] = dh
    near, far = keep.shape[:2]
    z, mine = place[0], place[1]
    step = 512
    each = step // (CORES * share)

    def parts_of(core):
        for k in range(width // step):
            rows = slice(k * step, (k + 1) * step)
            halves = (
                contract_rows(x[:, rows], dh).astype(BF16),
                contract_rows(g[:, rows], act).astype(BF16),
            )
            for n in range(each):
                away = lax.rem(k * each + n - z + near * far, near * far)
                r = lax.rem(away, near)
                for owner, out in ((core, keep), (1 - core, give)):
                    later = jnp.where(r == 3, 1, jnp.where(r == 2, owner, 0))
                    j = lax.rem(away // near + later, far)
                    at = slice((n * CORES + owner) * share, (n * CORES + owner + 1) * share)
                    out[r, j, :, :hidden] = halves[0][at]
                    out[r, j, :, hidden:] = halves[1][at]

    for core in range(CORES):
        pl.when(mine == core)(functools.partial(parts_of, core))


def expert(place, received, codes):
    width = received.shape[2]
    wide = codes.shape[2]
    share = codes.shape[1] - NOTE
    rows = EXPERTS * CAP
    whole = pl.BlockSpec(memory_space=pltpu.VMEM)
    chips = width // share // CORES
    near = 4
    return pl.pallas_call(
        expert_kernel,
        in_specs=[pl.BlockSpec(memory_space=pltpu.SMEM), whole, whole],
        out_specs=[whole] * 5,
        out_shape=[
            jax.ShapeDtypeStruct((rows, wide // 2), BF16),
            jax.ShapeDtypeStruct((rows, wide // 2), BF16),
            jax.ShapeDtypeStruct((width, wide), BF16),
            jax.ShapeDtypeStruct((near, chips // near, share, wide), BF16),
            jax.ShapeDtypeStruct((near, chips // near, share, wide), BF16),
        ],
        scratch_shapes=[
            pltpu.VMEM((rows, width), BF16),
            pltpu.VMEM((rows, width), BF16),
        ],
        compiler_params=pltpu.CompilerParams(vmem_limit_bytes=LARGE),
        name="expert",
    )(place, received, codes)


def return_kernel(act, dh, weights, back):
    hidden = weights.shape[1] // 2
    half = weights.shape[0] // 2
    body = EXPERTS * BODY
    rest = EXPERTS * REST
    over = []
    for kind, value in enumerate((act, dh)):
        for side in range(2):
            at = (2 * kind + side) * BODY
            weight = weights[side * half : (side + 1) * half, (1 - kind) * hidden : (2 - kind) * hidden]
            rows = contract_last(value[...], weight).astype(BF16)
            back[:, at : at + BODY, :] = rows[:body].reshape(EXPERTS, BODY, half)
            over.append(rows[body:])
    eight = 4 * REST
    spread = ones_where(
        EXPERTS * eight,
        4 * rest,
        lambda row: row % eight // REST * rest + row // eight * REST + row % REST,
    )
    over = dot(spread, jnp.concatenate(over, axis=0)).astype(BF16)
    back[:, 4 * BODY :, :] = over.reshape(EXPERTS, eight, half)


def returns(act, dh, weights):
    whole = pl.BlockSpec(memory_space=pltpu.VMEM)
    return pl.pallas_call(
        return_kernel,
        in_specs=[whole] * 3,
        out_specs=whole,
        out_shape=jax.ShapeDtypeStruct((EXPERTS, 4 * CAP, weights.shape[0] // 2), BF16),
        compiler_params=pltpu.CompilerParams(vmem_limit_bytes=LARGE),
        cost_estimate=LONG,
        name="returns",
    )(act, dh, weights)


def table_kernel(routes, gates, table, scale):
    number = routes.shape[1]
    first, second, count = named_and_earlier(routes[...])
    slot = lax.broadcasted_iota(jnp.int32, (1, BODY, number), 1)
    place = lax.broadcasted_iota(jnp.int32, (1, 4 * REST, number), 1)
    for k, chosen in enumerate((first, second, first | second)):
        held = jnp.where(chosen, count, -2)[:, None, :]
        body = jnp.where(held == slot, 1.0, 0.0).reshape(EXPERTS * BODY, number).T
        for side in range(2):
            start = REST * (2 * (k // 2) + side)
            mine = (place >= start) & (place < start + REST)
            over = jnp.where(mine & (held == place - start + BODY), 1.0, 0.0)
            over = over.reshape(EXPERTS * 4 * REST, number).T
            at = slice(k * number, (k + 1) * number)
            table[side, at] = jnp.concatenate([body, over], axis=1).astype(BF16)
    here = lax.broadcasted_iota(jnp.int32, (number, number), 0) == lax.broadcasted_iota(
        jnp.int32, (number, number), 1
    )
    for k in range(2):
        scale[k] = jnp.sum(jnp.where(here, gates[k : k + 1], 0.0), axis=1, keepdims=True)


def tables(routes, gates):
    number = routes.shape[1]
    return pl.pallas_call(
        table_kernel,
        out_shape=[
            jax.ShapeDtypeStruct((2, 3 * number, EXPERTS * (BODY + 4 * REST)), BF16),
            jax.ShapeDtypeStruct((2, number, 1), F32),
        ],
        compiler_params=pltpu.CompilerParams(vmem_limit_bytes=SMALL),
        cost_estimate=LONG,
        name="tables",
    )(routes, gates)


def combine_kernel(table, scale, back, mixed, input_grad):
    number = mixed.shape[0]
    half = back.shape[2]
    over = back[:, 4 * BODY :, :].reshape(EXPERTS * 4 * REST, half)
    for side in range(2):
        columns = slice(side * half, (side + 1) * half)
        kinds = []
        for kind in range(2):
            at = (2 * kind + side) * BODY
            body = back[:, at : at + BODY, :].reshape(EXPERTS * BODY, half)
            kinds.append(jnp.concatenate([body, over], axis=0))
        pairs = dot(table[side, : 2 * number], kinds[0])
        mixed[:, columns] = (scale[0] * pairs[:number] + scale[1] * pairs[number:]).astype(BF16)
        input_grad[:, columns] = dot(table[side, 2 * number :], kinds[1]).astype(BF16)


def combine(table, scale, back):
    number = scale.shape[1]
    width = 2 * back.shape[2]
    return pl.pallas_call(
        combine_kernel,
        out_shape=[jax.ShapeDtypeStruct((number, width), BF16)] * 2,
        compiler_params=pltpu.CompilerParams(vmem_limit_bytes=SMALL),
        name="combine",
    )(table, scale, back)


def local(chips, tokens, routes, gates, cotangent, up_weight, down_weight):
    near = 4
    far = chips // near

    def moved(array, hops):
        pairs = []
        for z in range(chips):
            for core in range(CORES):
                to = z * CORES + 1 - core if hops is None else (z + hops(core)) % chips * CORES + core
                pairs.append((z * CORES + core, to))
        return lax.ppermute(array, "dp", pairs)

    routes, gates = routes.T, gates.T
    send, codes = dispatch(routes, gates, tokens, cotangent, up_weight, down_weight)
    codes = lax.all_gather(codes.astype(jnp.float16), "dp").astype(BF16)
    received = lax.all_to_all(send, "expert", split_axis=0, concat_axis=0, tiled=True)
    me = lax.axis_index("dp").astype(jnp.int32)
    place = jnp.stack([me // CORES, me % CORES])
    act, dh, weights, keep, give = expert(place, received, codes)
    got = moved(give, None)

    def total(*arrays):
        return sum(a.astype(F32) for a in arrays)

    got, back = lax.optimization_barrier((got, returns(act, dh, weights)))
    quarter = total(keep[0], got[0])
    for r in range(1, near):
        chip_sum = total(keep[r], got[r]).astype(BF16)
        arrived = moved(chip_sum, lambda core: offset_of(r, core))
        quarter = quarter + arrived.astype(F32)
    quarter = quarter.astype(BF16)
    arrived = [moved(quarter[j], lambda core: near * j) for j in (1, 3, 2)]
    routes, gates, quarter = lax.optimization_barrier((routes, gates, quarter))
    table, scale = tables(routes, gates)
    back = lax.all_to_all(back, "expert", split_axis=0, concat_axis=0, tiled=True)
    mixed, input_grad = combine(table, scale, back)
    mixed, input_grad, arrived = lax.optimization_barrier((mixed, input_grad, arrived))
    hidden = up_weight.shape[2]
    up_grad, down_grad = (
        total(quarter[0][:, half], *[a[:, half] for a in arrived]).astype(BF16)[None]
        for half in (slice(0, hidden), slice(hidden, 2 * hidden))
    )
    return mixed, input_grad, up_grad, down_grad


def solution(mesh):
    token = P(("dp", "expert"), None)
    weight = P("expert", "dp", None)
    return jax.shard_map(
        functools.partial(local, mesh.shape["dp"] // CORES),
        mesh=mesh,
        in_specs=(token, token, token, token, weight, weight),
        out_specs=(token, token, weight, weight),
        check_vma=False,
    )
```

```python
import functools

import jax
import jax.numpy as jnp
from jax import lax
from jax.experimental import pallas as pl
from jax.experimental.pallas import tpu as pltpu
from jax.sharding import PartitionSpec as P

F32 = jnp.float32
BF16 = jnp.bfloat16
EXPERTS = 16
CAP = 18
BODY = 16
REST = CAP - BODY
BLOCK = 40
CORES = 2
NOTE = 8
SMALL = 16 * 1024 * 1024
LARGE = 40 * 1024 * 1024
WHOLE = 60 * 1024 * 1024
LONG = pl.CostEstimate(flops=50_000_000_000, bytes_accessed=1_000_000, transcendentals=0)


def dot(left, right):
    return lax.dot_general(left, right, (((1,), (0,)), ((), ())), preferred_element_type=F32)


def contract_rows(left, right):
    return lax.dot_general(left, right, (((0,), (0,)), ((), ())), preferred_element_type=F32)


def contract_last(left, right):
    return lax.dot_general(left, right, (((1,), (1,)), ((), ())), preferred_element_type=F32)


def named_and_earlier(routes):
    tokens = routes.shape[1]
    expert = lax.broadcasted_iota(jnp.int32, (EXPERTS, tokens), 0)
    first, second = expert == routes[0:1], expert == routes[1:2]
    earlier = lax.broadcasted_iota(jnp.int32, (tokens, tokens), 0) < lax.broadcasted_iota(
        jnp.int32, (tokens, tokens), 1
    )
    named = jnp.where(first | second, 1.0, 0.0).astype(BF16)
    count = dot(named, jnp.where(earlier, 1.0, 0.0).astype(BF16))
    return first, second, count.astype(jnp.int32)


def slots_of_rows(rows, lanes):
    row = lax.broadcasted_iota(jnp.int32, (1, rows, lanes), 1)
    one = jnp.where(row < BODY, row, -1)
    one = jnp.where((row >= 2 * BODY) & (row < 2 * BODY + REST), row - BODY, one)
    two = jnp.where((row >= BODY) & (row < 2 * BODY), row - BODY, -1)
    two = jnp.where((row >= 2 * BODY + REST) & (row < 2 * BODY + 2 * REST), row - BODY - REST, two)
    return one, two


def coded(weight):
    rows = weight.astype(F32)
    peak = jnp.max(jnp.max(jnp.abs(rows), axis=1, keepdims=True), axis=0, keepdims=True)
    power = jnp.floor(jnp.log2(16384.0 / jnp.maximum(peak, 2.0**-100)))
    factor = jnp.exp2(power).astype(BF16).astype(F32)
    code = (rows * factor).astype(BF16)
    return jnp.concatenate([code, jnp.broadcast_to(power, (NOTE, rows.shape[1])).astype(BF16)], axis=0)


def dispatch_kernel(
    routes, gates, up, down, tokens, cotangent, send, codes,
    routes_in, gates_in, up_in, down_in, both, table, rows, small_sems, in_sems, out_sems,
):
    number, width = tokens.shape
    steps, step = rows.shape[:2]
    small = [
        pltpu.make_async_copy(source, target, small_sems.at[k])
        for k, (source, target) in enumerate(
            ((routes, routes_in), (gates, gates_in), (up, up_in), (down, down_in))
        )
    ]
    large = [
        pltpu.make_async_copy(source, both.at[pl.ds(k * number, number)], in_sems.at[k])
        for k, source in enumerate((tokens, cotangent))
    ]
    for load in small + large:
        load.start()
    for load in small:
        load.wait()
    hidden = up.shape[2]
    codes[:, :hidden] = coded(up_in[0])
    codes[:, hidden:] = coded(down_in[0])
    first, second, count = named_and_earlier(routes_in[...])
    held = jnp.where(first | second, count, -2)[:, None, :]
    one, two = slots_of_rows(BLOCK, number)
    gate = jnp.where(first, gates_in[0:1], 0.0) + jnp.where(second, gates_in[1:2], 0.0)
    in_one, in_two = held == one, held == two
    table[:, :number] = jnp.where(in_one, 1.0, 0.0).reshape(EXPERTS * BLOCK, number).astype(BF16)
    table[:, number:] = jnp.where(in_two, 1.0, 0.0).reshape(EXPERTS * BLOCK, number).astype(BF16)
    scale = jnp.where(in_two, gate[:, None, :], 0.0) + jnp.where(in_one, 1.0, 0.0)
    scale = jnp.sum(scale.reshape(EXPERTS * BLOCK, number), axis=1, keepdims=True)
    for load in large:
        load.wait()
    stores = []
    for k in range(steps):
        at = slice(k * step * BLOCK, (k + 1) * step * BLOCK)
        block = dot(table[at], both[...]) * scale[at]
        rows[k] = block.astype(BF16).reshape(step, BLOCK, width)
        stores.append(
            pltpu.make_async_copy(rows.at[k], send.at[pl.ds(k * step, step)], out_sems.at[k])
        )
        stores[-1].start()
    for store in stores:
        store.wait()


def dispatch(routes, gates, tokens, cotangent, up_weight, down_weight):
    number, width = tokens.shape
    share, hidden = up_weight.shape[1:]
    step = 4
    steps = EXPERTS // step
    anywhere = pl.BlockSpec(memory_space=pl.ANY)
    return pl.pallas_call(
        dispatch_kernel,
        in_specs=[anywhere] * 6,
        out_specs=[anywhere, pl.BlockSpec(memory_space=pltpu.VMEM)],
        out_shape=[
            jax.ShapeDtypeStruct((EXPERTS, BLOCK, width), BF16),
            jax.ShapeDtypeStruct((share + NOTE, 2 * hidden), BF16),
        ],
        scratch_shapes=[
            pltpu.VMEM(routes.shape, jnp.int32),
            pltpu.VMEM(gates.shape, F32),
            pltpu.VMEM(up_weight.shape, BF16),
            pltpu.VMEM(down_weight.shape, BF16),
            pltpu.VMEM((2 * number, width), BF16),
            pltpu.VMEM((EXPERTS * BLOCK, 2 * number), BF16),
            pltpu.VMEM((steps, step, BLOCK, width), BF16),
            pltpu.SemaphoreType.DMA((4,)),
            pltpu.SemaphoreType.DMA((2,)),
            pltpu.SemaphoreType.DMA((steps,)),
        ],
        compiler_params=pltpu.CompilerParams(vmem_limit_bytes=WHOLE),
        name="dispatch",
    )(routes, gates, up_weight, down_weight, tokens, cotangent)


def offset_of(r, core):
    return (0, 1, 2 - 4 * core, -1)[r]


def ones_where(rows, columns, chosen):
    row = lax.broadcasted_iota(jnp.int32, (rows, columns), 0)
    column = lax.broadcasted_iota(jnp.int32, (rows, columns), 1)
    return jnp.where(chosen(row) == column, 1.0, 0.0).astype(BF16)


def expert_kernel(
    place, received, codes, act_out, dh_out, weights, keep, give, x, g
):
    width = received.shape[2]
    hidden = codes.shape[2] // 2
    share = codes.shape[1] - NOTE
    body = EXPERTS * BODY
    rest = EXPERTS * REST
    factor = jnp.exp2(-codes[:, share:, :].astype(F32)).astype(BF16)[:, :1, :]
    weights[...] = (codes[:, :share, :] * factor).reshape(weights.shape)
    x[:body] = received[:, :BODY, :].reshape(body, width)
    g[:body] = received[:, BODY : 2 * BODY, :].reshape(body, width)
    eight = BLOCK - 2 * BODY
    over = received[:, 2 * BODY :, :].reshape(EXPERTS * eight, width)
    pick = ones_where(
        2 * rest,
        EXPERTS * eight,
        lambda row: (row % rest) // REST * eight + row // rest * REST + row % REST,
    )
    over = dot(pick, over).astype(BF16)
    x[body:] = over[:rest]
    g[body:] = over[rest:]
    hpre = dot(x[...], weights[:, :hidden])
    dact = dot(g[...], weights[:, hidden:])
    s = 1.0 / (1.0 + jnp.exp(-hpre))
    act = (hpre * s).astype(BF16)
    dh = (dact * s * (1.0 + hpre * (1.0 - s))).astype(BF16)
    act_out[...] = act
    dh_out[...] = dh
    near, far = keep.shape[:2]
    z, mine = place[0], place[1]
    step = 512
    each = step // (CORES * share)

    def parts_of(core):
        for k in range(width // step):
            rows = slice(k * step, (k + 1) * step)
            halves = (
                contract_rows(x[:, rows], dh).astype(BF16),
                contract_rows(g[:, rows], act).astype(BF16),
            )
            for n in range(each):
                away = lax.rem(k * each + n - z + near * far, near * far)
                r = lax.rem(away, near)
                for owner, out in ((core, keep), (1 - core, give)):
                    later = jnp.where(r == 3, 1, jnp.where(r == 2, owner, 0))
                    j = lax.rem(away // near + later, far)
                    at = slice((n * CORES + owner) * share, (n * CORES + owner + 1) * share)
                    out[r, j, :, :hidden] = halves[0][at]
                    out[r, j, :, hidden:] = halves[1][at]

    for core in range(CORES):
        pl.when(mine == core)(functools.partial(parts_of, core))


def expert(place, received, codes):
    width = received.shape[2]
    wide = codes.shape[2]
    share = codes.shape[1] - NOTE
    rows = EXPERTS * CAP
    whole = pl.BlockSpec(memory_space=pltpu.VMEM)
    chips = width // share // CORES
    near = 4
    return pl.pallas_call(
        expert_kernel,
        in_specs=[pl.BlockSpec(memory_space=pltpu.SMEM), whole, whole],
        out_specs=[whole] * 5,
        out_shape=[
            jax.ShapeDtypeStruct((rows, wide // 2), BF16),
            jax.ShapeDtypeStruct((rows, wide // 2), BF16),
            jax.ShapeDtypeStruct((width, wide), BF16),
            jax.ShapeDtypeStruct((near, chips // near, share, wide), BF16),
            jax.ShapeDtypeStruct((near, chips // near, share, wide), BF16),
        ],
        scratch_shapes=[
            pltpu.VMEM((rows, width), BF16),
            pltpu.VMEM((rows, width), BF16),
        ],
        compiler_params=pltpu.CompilerParams(vmem_limit_bytes=LARGE),
        name="expert",
    )(place, received, codes)


def return_kernel(act, dh, weights, back):
    hidden = weights.shape[1] // 2
    half = weights.shape[0] // 2
    body = EXPERTS * BODY
    rest = EXPERTS * REST
    over = []
    for kind, value in enumerate((act, dh)):
        for side in range(2):
            at = (2 * kind + side) * BODY
            weight = weights[side * half : (side + 1) * half, (1 - kind) * hidden : (2 - kind) * hidden]
            rows = contract_last(value[...], weight).astype(BF16)
            back[:, at : at + BODY, :] = rows[:body].reshape(EXPERTS, BODY, half)
            over.append(rows[body:])
    eight = 4 * REST
    spread = ones_where(
        EXPERTS * eight,
        4 * rest,
        lambda row: row % eight // REST * rest + row // eight * REST + row % REST,
    )
    over = dot(spread, jnp.concatenate(over, axis=0)).astype(BF16)
    back[:, 4 * BODY :, :] = over.reshape(EXPERTS, eight, half)


def returns(act, dh, weights):
    whole = pl.BlockSpec(memory_space=pltpu.VMEM)
    return pl.pallas_call(
        return_kernel,
        in_specs=[whole] * 3,
        out_specs=whole,
        out_shape=jax.ShapeDtypeStruct((EXPERTS, 4 * CAP, weights.shape[0] // 2), BF16),
        compiler_params=pltpu.CompilerParams(vmem_limit_bytes=LARGE),
        cost_estimate=LONG,
        name="returns",
    )(act, dh, weights)


def table_kernel(routes, body, over):
    number = routes.shape[1]
    first, second, count = named_and_earlier(routes[...])
    slot = lax.broadcasted_iota(jnp.int32, (1, BODY, number), 1)
    place = lax.broadcasted_iota(jnp.int32, (1, 4 * REST, number), 1)
    for k, chosen in enumerate((first, second, first | second)):
        held = jnp.where(chosen, count, -2)[:, None, :]
        at = slice(k * number, (k + 1) * number)
        here = jnp.where(held == slot, 1.0, 0.0).reshape(EXPERTS * BODY, number)
        body[at] = here.T.astype(BF16)
        for side in range(2):
            start = REST * (2 * (k // 2) + side)
            mine = (place >= start) & (place < start + REST)
            here = jnp.where(mine & (held == place - start + BODY), 1.0, 0.0)
            over[side, at] = here.reshape(EXPERTS * 4 * REST, number).T.astype(BF16)


def tables(routes):
    number = routes.shape[1]
    return pl.pallas_call(
        table_kernel,
        out_shape=[
            jax.ShapeDtypeStruct((3 * number, EXPERTS * BODY), BF16),
            jax.ShapeDtypeStruct((2, 3 * number, EXPERTS * 4 * REST), BF16),
        ],
        compiler_params=pltpu.CompilerParams(vmem_limit_bytes=SMALL),
        name="tables",
    )(routes)


def combine_kernel(in_body, in_over, gates, back, mixed, input_grad):
    number = mixed.shape[0]
    half = back.shape[2]
    here = lax.broadcasted_iota(jnp.int32, (number, number), 0) == lax.broadcasted_iota(
        jnp.int32, (number, number), 1
    )
    gate = [
        jnp.sum(jnp.where(here, gates[k : k + 1], 0.0), axis=1, keepdims=True) for k in range(2)
    ]
    over = back[:, 4 * BODY :, :].reshape(EXPERTS * 4 * REST, half)

    def picked(at, kind, side):
        body = back[:, (2 * kind + side) * BODY : (2 * kind + side + 1) * BODY, :]
        return dot(
            jnp.concatenate([in_body[at], in_over[side, at]], axis=1),
            jnp.concatenate([body.reshape(EXPERTS * BODY, half), over], axis=0),
        )

    for side in range(2):
        columns = slice(side * half, (side + 1) * half)
        pairs = picked(slice(0, 2 * number), 0, side)
        mixed[:, columns] = (gate[0] * pairs[:number] + gate[1] * pairs[number:]).astype(BF16)
        input_grad[:, columns] = picked(slice(2 * number, 3 * number), 1, side).astype(BF16)


def combine(in_body, in_over, gates, back):
    number = gates.shape[1]
    width = 2 * back.shape[2]
    return pl.pallas_call(
        combine_kernel,
        out_shape=[jax.ShapeDtypeStruct((number, width), BF16)] * 2,
        compiler_params=pltpu.CompilerParams(vmem_limit_bytes=SMALL),
        name="combine",
    )(in_body, in_over, gates, back)


def partial_kernel(own, two, out):
    out[...] = own[...] + two[...].astype(F32)


def partial_sum(own, two):
    return pl.pallas_call(
        partial_kernel,
        out_shape=jax.ShapeDtypeStruct(two.shape, F32),
        compiler_params=pltpu.CompilerParams(vmem_limit_bytes=SMALL),
        cost_estimate=LONG,
        name="partial_sum",
    )(own, two)


def local(chips, tokens, routes, gates, cotangent, up_weight, down_weight):
    near = 4
    far = chips // near

    def moved(array, hops):
        pairs = []
        for z in range(chips):
            for core in range(CORES):
                to = z * CORES + 1 - core if hops is None else (z + hops(core)) % chips * CORES + core
                pairs.append((z * CORES + core, to))
        return lax.ppermute(array, "dp", pairs)

    routes, gates = routes.T, gates.T
    send, codes = dispatch(routes, gates, tokens, cotangent, up_weight, down_weight)
    codes = lax.all_gather(codes.astype(jnp.float16), "dp").astype(BF16)
    received = lax.all_to_all(send, "expert", split_axis=0, concat_axis=0, tiled=True)
    me = lax.axis_index("dp").astype(jnp.int32)
    place = jnp.stack([me // CORES, me % CORES])
    act, dh, weights, keep, give = expert(place, received, codes)
    got = moved(give, None)

    def total(*arrays):
        return sum(a.astype(F32) for a in arrays)

    got, back = lax.optimization_barrier((got, returns(act, dh, weights)))
    sums = [total(keep[r], got[r]) for r in range(near)]
    two = moved(sums[2].astype(BF16), lambda core: offset_of(2, core))
    partial = partial_sum(sums[0], two)
    routes, gates, partial = lax.optimization_barrier((routes, gates, partial))
    quarter = total(
        partial, *[moved(sums[r].astype(BF16), lambda core: offset_of(r, core)) for r in (1, 3)]
    )
    quarter = quarter.astype(BF16)
    arrived = [moved(quarter[j], lambda core: near * j) for j in (1, 3, 2)]
    in_body, in_over = tables(routes)
    back = lax.all_to_all(back, "expert", split_axis=0, concat_axis=0, tiled=True)
    mixed, input_grad = combine(in_body, in_over, gates, back)
    mixed, input_grad, arrived = lax.optimization_barrier((mixed, input_grad, arrived))
    hidden = up_weight.shape[2]
    up_grad, down_grad = (
        total(quarter[0][:, half], *[a[:, half] for a in arrived]).astype(BF16)[None]
        for half in (slice(0, hidden), slice(hidden, 2 * hidden))
    )
    return mixed, input_grad, up_grad, down_grad


def solution(mesh):
    token = P(("dp", "expert"), None)
    weight = P("expert", "dp", None)
    return jax.shard_map(
        functools.partial(local, mesh.shape["dp"] // CORES),
        mesh=mesh,
        in_specs=(token, token, token, token, weight, weight),
        out_specs=(token, token, weight, weight),
        check_vma=False,
    )
```

```python
import functools

import jax
import jax.numpy as jnp
from jax import lax
from jax.experimental import pallas as pl
from jax.experimental.pallas import tpu as pltpu
from jax.sharding import PartitionSpec as P

F32 = jnp.float32
BF16 = jnp.bfloat16
EXPERTS = 16
CAP = 18
BODY = 16
REST = CAP - BODY
BLOCK = 40
CORES = 2
NOTE = 8
SMALL = 16 * 1024 * 1024
LARGE = 40 * 1024 * 1024
WHOLE = 60 * 1024 * 1024
LONG = pl.CostEstimate(flops=50_000_000_000, bytes_accessed=1_000_000, transcendentals=0)


def dot(left, right):
    return lax.dot_general(left, right, (((1,), (0,)), ((), ())), preferred_element_type=F32)


def contract_rows(left, right):
    return lax.dot_general(left, right, (((0,), (0,)), ((), ())), preferred_element_type=F32)


def contract_last(left, right):
    return lax.dot_general(left, right, (((1,), (1,)), ((), ())), preferred_element_type=F32)


def named_and_earlier(routes):
    tokens = routes.shape[1]
    expert = lax.broadcasted_iota(jnp.int32, (EXPERTS, tokens), 0)
    first, second = expert == routes[0:1], expert == routes[1:2]
    earlier = lax.broadcasted_iota(jnp.int32, (tokens, tokens), 0) < lax.broadcasted_iota(
        jnp.int32, (tokens, tokens), 1
    )
    named = jnp.where(first | second, 1.0, 0.0).astype(BF16)
    count = dot(named, jnp.where(earlier, 1.0, 0.0).astype(BF16))
    return first, second, count.astype(jnp.int32)


def slots_of_rows(rows, lanes):
    row = lax.broadcasted_iota(jnp.int32, (1, rows, lanes), 1)
    one = jnp.where(row < BODY, row, -1)
    one = jnp.where((row >= 2 * BODY) & (row < 2 * BODY + REST), row - BODY, one)
    two = jnp.where((row >= BODY) & (row < 2 * BODY), row - BODY, -1)
    two = jnp.where((row >= 2 * BODY + REST) & (row < 2 * BODY + 2 * REST), row - BODY - REST, two)
    return one, two


def coded(weight):
    rows = weight.astype(F32)
    peak = jnp.max(jnp.max(jnp.abs(rows), axis=1, keepdims=True), axis=0, keepdims=True)
    power = jnp.floor(jnp.log2(16384.0 / jnp.maximum(peak, 2.0**-100)))
    factor = jnp.exp2(power).astype(BF16).astype(F32)
    code = (rows * factor).astype(BF16)
    return jnp.concatenate([code, jnp.broadcast_to(power, (NOTE, rows.shape[1])).astype(BF16)], axis=0)


def dispatch_kernel(
    routes, gates, up, down, tokens, cotangent, send, codes,
    routes_in, gates_in, up_in, down_in, both, table, rows, small_sems, in_sems, out_sems,
):
    number, width = tokens.shape
    steps, step = rows.shape[:2]
    small = [
        pltpu.make_async_copy(source, target, small_sems.at[k])
        for k, (source, target) in enumerate(
            ((routes, routes_in), (gates, gates_in), (up, up_in), (down, down_in))
        )
    ]
    large = [
        pltpu.make_async_copy(source, both.at[pl.ds(k * number, number)], in_sems.at[k])
        for k, source in enumerate((tokens, cotangent))
    ]
    for load in small + large:
        load.start()
    for load in small:
        load.wait()
    hidden = up.shape[2]
    codes[:, :hidden] = coded(up_in[0])
    codes[:, hidden:] = coded(down_in[0])
    first, second, count = named_and_earlier(routes_in[...])
    held = jnp.where(first | second, count, -2)[:, None, :]
    one, two = slots_of_rows(BLOCK, number)
    gate = jnp.where(first, gates_in[0:1], 0.0) + jnp.where(second, gates_in[1:2], 0.0)
    in_one, in_two = held == one, held == two
    table[:, :number] = jnp.where(in_one, 1.0, 0.0).reshape(EXPERTS * BLOCK, number).astype(BF16)
    table[:, number:] = jnp.where(in_two, 1.0, 0.0).reshape(EXPERTS * BLOCK, number).astype(BF16)
    scale = jnp.where(in_two, gate[:, None, :], 0.0) + jnp.where(in_one, 1.0, 0.0)
    scale = jnp.sum(scale.reshape(EXPERTS * BLOCK, number), axis=1, keepdims=True)
    for load in large:
        load.wait()
    stores = []
    for k in range(steps):
        at = slice(k * step * BLOCK, (k + 1) * step * BLOCK)
        block = dot(table[at], both[...]) * scale[at]
        rows[k] = block.astype(BF16).reshape(step, BLOCK, width)
        stores.append(
            pltpu.make_async_copy(rows.at[k], send.at[pl.ds(k * step, step)], out_sems.at[k])
        )
        stores[-1].start()
    for store in stores:
        store.wait()


def dispatch(routes, gates, tokens, cotangent, up_weight, down_weight):
    number, width = tokens.shape
    share, hidden = up_weight.shape[1:]
    step = 4
    steps = EXPERTS // step
    anywhere = pl.BlockSpec(memory_space=pl.ANY)
    return pl.pallas_call(
        dispatch_kernel,
        in_specs=[anywhere] * 6,
        out_specs=[anywhere, pl.BlockSpec(memory_space=pltpu.VMEM)],
        out_shape=[
            jax.ShapeDtypeStruct((EXPERTS, BLOCK, width), BF16),
            jax.ShapeDtypeStruct((share + NOTE, 2 * hidden), BF16),
        ],
        scratch_shapes=[
            pltpu.VMEM(routes.shape, jnp.int32),
            pltpu.VMEM(gates.shape, F32),
            pltpu.VMEM(up_weight.shape, BF16),
            pltpu.VMEM(down_weight.shape, BF16),
            pltpu.VMEM((2 * number, width), BF16),
            pltpu.VMEM((EXPERTS * BLOCK, 2 * number), BF16),
            pltpu.VMEM((steps, step, BLOCK, width), BF16),
            pltpu.SemaphoreType.DMA((4,)),
            pltpu.SemaphoreType.DMA((2,)),
            pltpu.SemaphoreType.DMA((steps,)),
        ],
        compiler_params=pltpu.CompilerParams(vmem_limit_bytes=WHOLE),
        name="dispatch",
    )(routes, gates, up_weight, down_weight, tokens, cotangent)


def ones_where(rows, columns, chosen):
    row = lax.broadcasted_iota(jnp.int32, (rows, columns), 0)
    column = lax.broadcasted_iota(jnp.int32, (rows, columns), 1)
    return jnp.where(chosen(row) == column, 1.0, 0.0).astype(BF16)


def expert_kernel(
    place, received, codes, act_out, dh_out, weights, keep, give, x, g
):
    width = received.shape[2]
    hidden = codes.shape[2] // 2
    share = codes.shape[1] - NOTE
    body = EXPERTS * BODY
    rest = EXPERTS * REST
    factor = jnp.exp2(-codes[:, share:, :].astype(F32)).astype(BF16)[:, :1, :]
    weights[...] = (codes[:, :share, :] * factor).reshape(weights.shape)
    x[:body] = received[:, :BODY, :].reshape(body, width)
    g[:body] = received[:, BODY : 2 * BODY, :].reshape(body, width)
    eight = BLOCK - 2 * BODY
    over = received[:, 2 * BODY :, :].reshape(EXPERTS * eight, width)
    pick = ones_where(
        2 * rest,
        EXPERTS * eight,
        lambda row: (row % rest) // REST * eight + row // rest * REST + row % REST,
    )
    over = dot(pick, over).astype(BF16)
    x[body:] = over[:rest]
    g[body:] = over[rest:]
    hpre = dot(x[...], weights[:, :hidden])
    dact = dot(g[...], weights[:, hidden:])
    s = 1.0 / (1.0 + jnp.exp(-hpre))
    act = (hpre * s).astype(BF16)
    dh = (dact * s * (1.0 + hpre * (1.0 - s))).astype(BF16)
    act_out[...] = act
    dh_out[...] = dh
    near, far = keep.shape[:2]
    z, mine = place[0], place[1]
    step = 512
    each = step // (CORES * share)

    def parts_of(core):
        for k in range(width // step):
            rows = slice(k * step, (k + 1) * step)
            halves = (
                contract_rows(x[:, rows], dh).astype(BF16),
                contract_rows(g[:, rows], act).astype(BF16),
            )
            for n in range(each):
                away = lax.rem(k * each + n - z + near * far, near * far)
                r = lax.rem(away, near)
                for owner, out in ((core, keep), (1 - core, give)):
                    later = jnp.where(r == 3, 1, jnp.where(r == 2, owner, 0))
                    j = lax.rem(away // near + later, far)
                    to = (r, j)
                    if owner == 1:
                        to = (lax.rem(near - r, near), lax.rem(far - j, far))
                    at = slice((n * CORES + owner) * share, (n * CORES + owner + 1) * share)
                    out[(*to, slice(None), slice(0, hidden))] = halves[0][at]
                    out[(*to, slice(None), slice(hidden, 2 * hidden))] = halves[1][at]

    for core in range(CORES):
        pl.when(mine == core)(functools.partial(parts_of, core))


def expert(place, received, codes):
    width = received.shape[2]
    wide = codes.shape[2]
    share = codes.shape[1] - NOTE
    rows = EXPERTS * CAP
    whole = pl.BlockSpec(memory_space=pltpu.VMEM)
    chips = width // share // CORES
    near = 4
    return pl.pallas_call(
        expert_kernel,
        in_specs=[pl.BlockSpec(memory_space=pltpu.SMEM), whole, whole],
        out_specs=[whole] * 5,
        out_shape=[
            jax.ShapeDtypeStruct((rows, wide // 2), BF16),
            jax.ShapeDtypeStruct((rows, wide // 2), BF16),
            jax.ShapeDtypeStruct((width, wide), BF16),
            jax.ShapeDtypeStruct((near, chips // near, share, wide), BF16),
            jax.ShapeDtypeStruct((near, chips // near, share, wide), BF16),
        ],
        scratch_shapes=[
            pltpu.VMEM((rows, width), BF16),
            pltpu.VMEM((rows, width), BF16),
        ],
        compiler_params=pltpu.CompilerParams(vmem_limit_bytes=LARGE),
        name="expert",
    )(place, received, codes)


def return_kernel(act, dh, weights, back):
    hidden = weights.shape[1] // 2
    half = weights.shape[0] // 2
    body = EXPERTS * BODY
    rest = EXPERTS * REST
    over = []
    for kind, value in enumerate((act, dh)):
        for side in range(2):
            at = (2 * kind + side) * BODY
            weight = weights[side * half : (side + 1) * half, (1 - kind) * hidden : (2 - kind) * hidden]
            rows = contract_last(value[...], weight).astype(BF16)
            back[:, at : at + BODY, :] = rows[:body].reshape(EXPERTS, BODY, half)
            over.append(rows[body:])
    eight = 4 * REST
    spread = ones_where(
        EXPERTS * eight,
        4 * rest,
        lambda row: row % eight // REST * rest + row // eight * REST + row % REST,
    )
    over = dot(spread, jnp.concatenate(over, axis=0)).astype(BF16)
    back[:, 4 * BODY :, :] = over.reshape(EXPERTS, eight, half)


def returns(act, dh, weights):
    whole = pl.BlockSpec(memory_space=pltpu.VMEM)
    return pl.pallas_call(
        return_kernel,
        in_specs=[whole] * 3,
        out_specs=whole,
        out_shape=jax.ShapeDtypeStruct((EXPERTS, 4 * CAP, weights.shape[0] // 2), BF16),
        compiler_params=pltpu.CompilerParams(vmem_limit_bytes=LARGE),
        cost_estimate=LONG,
        name="returns",
    )(act, dh, weights)


def table_kernel(routes, body, over):
    number = routes.shape[1]
    first, second, count = named_and_earlier(routes[...])
    slot = lax.broadcasted_iota(jnp.int32, (1, BODY, number), 1)
    place = lax.broadcasted_iota(jnp.int32, (1, 4 * REST, number), 1)
    for k, chosen in enumerate((first, second, first | second)):
        held = jnp.where(chosen, count, -2)[:, None, :]
        at = slice(k * number, (k + 1) * number)
        here = jnp.where(held == slot, 1.0, 0.0).reshape(EXPERTS * BODY, number)
        body[at] = here.T.astype(BF16)
        for side in range(2):
            start = REST * (2 * (k // 2) + side)
            mine = (place >= start) & (place < start + REST)
            here = jnp.where(mine & (held == place - start + BODY), 1.0, 0.0)
            over[side, at] = here.reshape(EXPERTS * 4 * REST, number).T.astype(BF16)


def tables(routes):
    number = routes.shape[1]
    return pl.pallas_call(
        table_kernel,
        out_shape=[
            jax.ShapeDtypeStruct((3 * number, EXPERTS * BODY), BF16),
            jax.ShapeDtypeStruct((2, 3 * number, EXPERTS * 4 * REST), BF16),
        ],
        compiler_params=pltpu.CompilerParams(vmem_limit_bytes=SMALL),
        name="tables",
    )(routes)


def combine_kernel(in_body, in_over, gates, back, mixed, input_grad):
    number = mixed.shape[0]
    half = back.shape[2]
    here = lax.broadcasted_iota(jnp.int32, (number, number), 0) == lax.broadcasted_iota(
        jnp.int32, (number, number), 1
    )
    gate = [
        jnp.sum(jnp.where(here, gates[k : k + 1], 0.0), axis=1, keepdims=True) for k in range(2)
    ]
    over = back[:, 4 * BODY :, :].reshape(EXPERTS * 4 * REST, half)

    def picked(at, kind, side):
        body = back[:, (2 * kind + side) * BODY : (2 * kind + side + 1) * BODY, :]
        return dot(
            jnp.concatenate([in_body[at], in_over[side, at]], axis=1),
            jnp.concatenate([body.reshape(EXPERTS * BODY, half), over], axis=0),
        )

    for side in range(2):
        columns = slice(side * half, (side + 1) * half)
        pairs = picked(slice(0, 2 * number), 0, side)
        mixed[:, columns] = (gate[0] * pairs[:number] + gate[1] * pairs[number:]).astype(BF16)
        input_grad[:, columns] = picked(slice(2 * number, 3 * number), 1, side).astype(BF16)


def combine(in_body, in_over, gates, back):
    number = gates.shape[1]
    width = 2 * back.shape[2]
    return pl.pallas_call(
        combine_kernel,
        out_shape=[jax.ShapeDtypeStruct((number, width), BF16)] * 2,
        compiler_params=pltpu.CompilerParams(vmem_limit_bytes=SMALL),
        name="combine",
    )(in_body, in_over, gates, back)


def partial_kernel(own, two, out):
    out[...] = own[...] + two[...].astype(F32)


def partial_sum(own, two):
    return pl.pallas_call(
        partial_kernel,
        out_shape=jax.ShapeDtypeStruct(two.shape, F32),
        compiler_params=pltpu.CompilerParams(vmem_limit_bytes=SMALL),
        cost_estimate=LONG,
        name="partial_sum",
    )(own, two)


def local(chips, tokens, routes, gates, cotangent, up_weight, down_weight):
    near = 4
    far = chips // near

    def moved(array, hops):
        pairs = []
        for z in range(chips):
            for core in range(CORES):
                to = z * CORES + 1 - core if hops is None else (z + hops(core)) % chips * CORES + core
                pairs.append((z * CORES + core, to))
        return lax.ppermute(array, "dp", pairs)

    routes, gates = routes.T, gates.T
    send, codes = dispatch(routes, gates, tokens, cotangent, up_weight, down_weight)
    codes = lax.all_gather(codes.astype(jnp.float16), "dp").astype(BF16)
    received = lax.all_to_all(send, "expert", split_axis=0, concat_axis=0, tiled=True)
    me = lax.axis_index("dp").astype(jnp.int32)
    place = jnp.stack([me // CORES, me % CORES])
    act, dh, weights, keep, give = expert(place, received, codes)
    got = moved(give, None)

    def total(*arrays):
        return sum(a.astype(F32) for a in arrays)

    got, back = lax.optimization_barrier((got, returns(act, dh, weights)))
    sums = [total(keep[r], got[r]) for r in range(near)]
    two = moved(sums[2].astype(BF16), lambda core: 2 - 4 * core)
    partial = partial_sum(sums[0], two)
    routes, gates, partial = lax.optimization_barrier((routes, gates, partial))
    def both_ways(ahead, behind, steps):
        turn = lambda core: steps * (1 - 2 * core)
        return moved(ahead, turn), moved(behind, lambda core: -turn(core))

    near_sums = both_ways(sums[1].astype(BF16), sums[3].astype(BF16), 1)
    quarter = total(partial, *near_sums).astype(BF16)
    arrived = [
        *both_ways(quarter[1], quarter[3], near),
        moved(quarter[2], lambda core: 2 * near),
    ]
    in_body, in_over = tables(routes)
    back = lax.all_to_all(back, "expert", split_axis=0, concat_axis=0, tiled=True)
    mixed, input_grad = combine(in_body, in_over, gates, back)
    mixed, input_grad, arrived = lax.optimization_barrier((mixed, input_grad, arrived))
    hidden = up_weight.shape[2]
    up_grad, down_grad = (
        total(quarter[0][:, half], *[a[:, half] for a in arrived]).astype(BF16)[None]
        for half in (slice(0, hidden), slice(hidden, 2 * hidden))
    )
    return mixed, input_grad, up_grad, down_grad


def solution(mesh):
    token = P(("dp", "expert"), None)
    weight = P("expert", "dp", None)
    return jax.shard_map(
        functools.partial(local, mesh.shape["dp"] // CORES),
        mesh=mesh,
        in_specs=(token, token, token, token, weight, weight),
        out_specs=(token, token, weight, weight),
        check_vma=False,
    )
```

```python
import functools

import jax
import jax.numpy as jnp
from jax import lax
from jax.experimental import pallas as pl
from jax.experimental.pallas import tpu as pltpu
from jax.sharding import PartitionSpec as P

F32 = jnp.float32
BF16 = jnp.bfloat16
EXPERTS = 16
CAP = 18
BODY = 16
REST = CAP - BODY
BLOCK = 40
CORES = 2
NOTE = 8
SMALL = 16 * 1024 * 1024
LARGE = 40 * 1024 * 1024
WHOLE = 60 * 1024 * 1024
LONG = pl.CostEstimate(flops=50_000_000_000, bytes_accessed=1_000_000, transcendentals=0)


def dot(left, right):
    return lax.dot_general(left, right, (((1,), (0,)), ((), ())), preferred_element_type=F32)


def contract_rows(left, right):
    return lax.dot_general(left, right, (((0,), (0,)), ((), ())), preferred_element_type=F32)


def contract_last(left, right):
    return lax.dot_general(left, right, (((1,), (1,)), ((), ())), preferred_element_type=F32)


def named_and_earlier(routes):
    tokens = routes.shape[1]
    expert = lax.broadcasted_iota(jnp.int32, (EXPERTS, tokens), 0)
    first, second = expert == routes[0:1], expert == routes[1:2]
    earlier = lax.broadcasted_iota(jnp.int32, (tokens, tokens), 0) < lax.broadcasted_iota(
        jnp.int32, (tokens, tokens), 1
    )
    named = jnp.where(first | second, 1.0, 0.0).astype(BF16)
    count = dot(named, jnp.where(earlier, 1.0, 0.0).astype(BF16))
    return first, second, count.astype(jnp.int32)


def slots_of_rows(rows, lanes):
    row = lax.broadcasted_iota(jnp.int32, (1, rows, lanes), 1)
    one = jnp.where(row < BODY, row, -1)
    one = jnp.where((row >= 2 * BODY) & (row < 2 * BODY + REST), row - BODY, one)
    two = jnp.where((row >= BODY) & (row < 2 * BODY), row - BODY, -1)
    two = jnp.where((row >= 2 * BODY + REST) & (row < 2 * BODY + 2 * REST), row - BODY - REST, two)
    return one, two


def coded(weight):
    rows = weight.astype(F32)
    peak = jnp.max(jnp.max(jnp.abs(rows), axis=1, keepdims=True), axis=0, keepdims=True)
    power = jnp.floor(jnp.log2(16384.0 / jnp.maximum(peak, 2.0**-100)))
    factor = jnp.exp2(power).astype(BF16).astype(F32)
    return (rows * factor).astype(BF16), power


def dispatch_kernel(
    routes, gates, up, down, tokens, cotangent, send, codes,
    routes_in, gates_in, up_in, down_in, both, table, rows, small_sems, in_sems, out_sems,
):
    number, width = tokens.shape
    steps, step = rows.shape[:2]
    small = [
        pltpu.make_async_copy(source, target, small_sems.at[k])
        for k, (source, target) in enumerate(
            ((routes, routes_in), (gates, gates_in), (up, up_in), (down, down_in))
        )
    ]
    large = [
        pltpu.make_async_copy(source, both.at[pl.ds(k * number, number)], in_sems.at[k])
        for k, source in enumerate((tokens, cotangent))
    ]
    for load in small + large:
        load.start()
    for load in small:
        load.wait()
    share, hidden = up.shape[1:]
    codes[:share], up_power = coded(up_in[0])
    codes[share : 2 * share], down_power = coded(down_in[0])
    note = lax.broadcasted_iota(jnp.int32, (NOTE, hidden), 0) < NOTE // 2
    codes[2 * share :] = jnp.where(note, up_power, down_power).astype(BF16)
    first, second, count = named_and_earlier(routes_in[...])
    held = jnp.where(first | second, count, -2)[:, None, :]
    one, two = slots_of_rows(BLOCK, number)
    gate = jnp.where(first, gates_in[0:1], 0.0) + jnp.where(second, gates_in[1:2], 0.0)
    in_one, in_two = held == one, held == two
    table[:, :number] = jnp.where(in_one, 1.0, 0.0).reshape(EXPERTS * BLOCK, number).astype(BF16)
    table[:, number:] = jnp.where(in_two, 1.0, 0.0).reshape(EXPERTS * BLOCK, number).astype(BF16)
    scale = jnp.where(in_two, gate[:, None, :], 0.0) + jnp.where(in_one, 1.0, 0.0)
    scale = jnp.sum(scale.reshape(EXPERTS * BLOCK, number), axis=1, keepdims=True)
    for load in large:
        load.wait()
    stores = []
    for k in range(steps):
        at = slice(k * step * BLOCK, (k + 1) * step * BLOCK)
        block = dot(table[at], both[...]) * scale[at]
        rows[k] = block.astype(BF16).reshape(step, BLOCK, width)
        stores.append(
            pltpu.make_async_copy(rows.at[k], send.at[pl.ds(k * step, step)], out_sems.at[k])
        )
        stores[-1].start()
    for store in stores:
        store.wait()


def dispatch(routes, gates, tokens, cotangent, up_weight, down_weight):
    number, width = tokens.shape
    share, hidden = up_weight.shape[1:]
    step = 4
    steps = EXPERTS // step
    anywhere = pl.BlockSpec(memory_space=pl.ANY)
    return pl.pallas_call(
        dispatch_kernel,
        in_specs=[anywhere] * 6,
        out_specs=[anywhere, pl.BlockSpec(memory_space=pltpu.VMEM)],
        out_shape=[
            jax.ShapeDtypeStruct((EXPERTS, BLOCK, width), BF16),
            jax.ShapeDtypeStruct((2 * share + NOTE, hidden), BF16),
        ],
        scratch_shapes=[
            pltpu.VMEM(routes.shape, jnp.int32),
            pltpu.VMEM(gates.shape, F32),
            pltpu.VMEM(up_weight.shape, BF16),
            pltpu.VMEM(down_weight.shape, BF16),
            pltpu.VMEM((2 * number, width), BF16),
            pltpu.VMEM((EXPERTS * BLOCK, 2 * number), BF16),
            pltpu.VMEM((steps, step, BLOCK, width), BF16),
            pltpu.SemaphoreType.DMA((4,)),
            pltpu.SemaphoreType.DMA((2,)),
            pltpu.SemaphoreType.DMA((steps,)),
        ],
        compiler_params=pltpu.CompilerParams(vmem_limit_bytes=WHOLE),
        name="dispatch",
    )(routes, gates, up_weight, down_weight, tokens, cotangent)


def ones_where(rows, columns, chosen):
    row = lax.broadcasted_iota(jnp.int32, (rows, columns), 0)
    column = lax.broadcasted_iota(jnp.int32, (rows, columns), 1)
    return jnp.where(chosen(row) == column, 1.0, 0.0).astype(BF16)


def expert_kernel(
    place, received, codes, act_out, dh_out, weights, keep, give, x, g
):
    width = received.shape[2]
    hidden = codes.shape[2]
    share = (codes.shape[1] - NOTE) // 2
    body = EXPERTS * BODY
    rest = EXPERTS * REST
    factor = jnp.exp2(-codes[:, 2 * share :, :].astype(F32)).astype(BF16)
    for n in range(2):
        rows = codes[:, n * share : (n + 1) * share, :]
        here = factor[:, n * NOTE // 2 : n * NOTE // 2 + 1, :]
        weights[:, n * hidden : (n + 1) * hidden] = (rows * here).reshape(width, hidden)
    x[:body] = received[:, :BODY, :].reshape(body, width)
    g[:body] = received[:, BODY : 2 * BODY, :].reshape(body, width)
    eight = BLOCK - 2 * BODY
    over = received[:, 2 * BODY :, :].reshape(EXPERTS * eight, width)
    pick = ones_where(
        2 * rest,
        EXPERTS * eight,
        lambda row: (row % rest) // REST * eight + row // rest * REST + row % REST,
    )
    over = dot(pick, over).astype(BF16)
    x[body:] = over[:rest]
    g[body:] = over[rest:]
    hpre = dot(x[...], weights[:, :hidden])
    dact = dot(g[...], weights[:, hidden:])
    s = 1.0 / (1.0 + jnp.exp(-hpre))
    act = (hpre * s).astype(BF16)
    dh = (dact * s * (1.0 + hpre * (1.0 - s))).astype(BF16)
    act_out[...] = act
    dh_out[...] = dh
    near, far = keep.shape[:2]
    z, mine = place[0], place[1]
    step = 512
    each = step // (CORES * share)

    def parts_of(core):
        for k in range(width // step):
            rows = slice(k * step, (k + 1) * step)
            halves = (
                contract_rows(x[:, rows], dh).astype(BF16),
                contract_rows(g[:, rows], act).astype(BF16),
            )
            for n in range(each):
                away = lax.rem(k * each + n - z + near * far, near * far)
                r = lax.rem(away, near)
                for owner, out in ((core, keep), (1 - core, give)):
                    later = jnp.where(r == 3, 1, jnp.where(r == 2, owner, 0))
                    j = lax.rem(away // near + later, far)
                    to = (r, j)
                    if owner == 1:
                        to = (lax.rem(near - r, near), lax.rem(far - j, far))
                    at = slice((n * CORES + owner) * share, (n * CORES + owner + 1) * share)
                    out[(*to, slice(None), slice(0, hidden))] = halves[0][at]
                    out[(*to, slice(None), slice(hidden, 2 * hidden))] = halves[1][at]

    for core in range(CORES):
        pl.when(mine == core)(functools.partial(parts_of, core))


def expert(place, received, codes):
    width = received.shape[2]
    wide = 2 * codes.shape[2]
    share = (codes.shape[1] - NOTE) // 2
    rows = EXPERTS * CAP
    whole = pl.BlockSpec(memory_space=pltpu.VMEM)
    chips = width // share // CORES
    near = 4
    return pl.pallas_call(
        expert_kernel,
        in_specs=[pl.BlockSpec(memory_space=pltpu.SMEM), whole, whole],
        out_specs=[whole] * 5,
        out_shape=[
            jax.ShapeDtypeStruct((rows, wide // 2), BF16),
            jax.ShapeDtypeStruct((rows, wide // 2), BF16),
            jax.ShapeDtypeStruct((width, wide), BF16),
            jax.ShapeDtypeStruct((near, chips // near, share, wide), BF16),
            jax.ShapeDtypeStruct((near, chips // near, share, wide), BF16),
        ],
        scratch_shapes=[
            pltpu.VMEM((rows, width), BF16),
            pltpu.VMEM((rows, width), BF16),
        ],
        compiler_params=pltpu.CompilerParams(vmem_limit_bytes=LARGE),
        name="expert",
    )(place, received, codes)


def return_kernel(act, dh, weights, back):
    hidden = weights.shape[1] // 2
    half = weights.shape[0] // 2
    body = EXPERTS * BODY
    rest = EXPERTS * REST
    over = []
    for kind, value in enumerate((act, dh)):
        for side in range(2):
            at = (2 * kind + side) * BODY
            weight = weights[side * half : (side + 1) * half, (1 - kind) * hidden : (2 - kind) * hidden]
            rows = contract_last(value[...], weight).astype(BF16)
            back[:, at : at + BODY, :] = rows[:body].reshape(EXPERTS, BODY, half)
            over.append(rows[body:])
    eight = 4 * REST
    spread = ones_where(
        EXPERTS * eight,
        4 * rest,
        lambda row: row % eight // REST * rest + row // eight * REST + row % REST,
    )
    over = dot(spread, jnp.concatenate(over, axis=0)).astype(BF16)
    back[:, 4 * BODY :, :] = over.reshape(EXPERTS, eight, half)


def returns(act, dh, weights):
    whole = pl.BlockSpec(memory_space=pltpu.VMEM)
    return pl.pallas_call(
        return_kernel,
        in_specs=[whole] * 3,
        out_specs=whole,
        out_shape=jax.ShapeDtypeStruct((EXPERTS, 4 * CAP, weights.shape[0] // 2), BF16),
        compiler_params=pltpu.CompilerParams(vmem_limit_bytes=LARGE),
        cost_estimate=LONG,
        name="returns",
    )(act, dh, weights)


def table_kernel(routes, body, over):
    number = routes.shape[1]
    first, second, count = named_and_earlier(routes[...])
    slot = lax.broadcasted_iota(jnp.int32, (1, BODY, number), 1)
    place = lax.broadcasted_iota(jnp.int32, (1, 4 * REST, number), 1)
    for k, chosen in enumerate((first, second, first | second)):
        held = jnp.where(chosen, count, -2)[:, None, :]
        at = slice(k * number, (k + 1) * number)
        here = jnp.where(held == slot, 1.0, 0.0).reshape(EXPERTS * BODY, number)
        body[at] = here.T.astype(BF16)
        for side in range(2):
            start = REST * (2 * (k // 2) + side)
            mine = (place >= start) & (place < start + REST)
            here = jnp.where(mine & (held == place - start + BODY), 1.0, 0.0)
            over[side, at] = here.reshape(EXPERTS * 4 * REST, number).T.astype(BF16)


def tables(routes):
    number = routes.shape[1]
    return pl.pallas_call(
        table_kernel,
        out_shape=[
            jax.ShapeDtypeStruct((3 * number, EXPERTS * BODY), BF16),
            jax.ShapeDtypeStruct((2, 3 * number, EXPERTS * 4 * REST), BF16),
        ],
        compiler_params=pltpu.CompilerParams(vmem_limit_bytes=SMALL),
        name="tables",
    )(routes)


def combine_kernel(in_body, in_over, gates, back, mixed, input_grad):
    number = mixed.shape[0]
    half = back.shape[2]
    here = lax.broadcasted_iota(jnp.int32, (number, number), 0) == lax.broadcasted_iota(
        jnp.int32, (number, number), 1
    )
    gate = [
        jnp.sum(jnp.where(here, gates[k : k + 1], 0.0), axis=1, keepdims=True) for k in range(2)
    ]
    over = back[:, 4 * BODY :, :].reshape(EXPERTS * 4 * REST, half)

    def picked(at, kind, side):
        body = back[:, (2 * kind + side) * BODY : (2 * kind + side + 1) * BODY, :]
        return dot(
            jnp.concatenate([in_body[at], in_over[side, at]], axis=1),
            jnp.concatenate([body.reshape(EXPERTS * BODY, half), over], axis=0),
        )

    for side in range(2):
        columns = slice(side * half, (side + 1) * half)
        pairs = picked(slice(0, 2 * number), 0, side)
        mixed[:, columns] = (gate[0] * pairs[:number] + gate[1] * pairs[number:]).astype(BF16)
        input_grad[:, columns] = picked(slice(2 * number, 3 * number), 1, side).astype(BF16)


def combine(in_body, in_over, gates, back):
    number = gates.shape[1]
    width = 2 * back.shape[2]
    return pl.pallas_call(
        combine_kernel,
        out_shape=[jax.ShapeDtypeStruct((number, width), BF16)] * 2,
        compiler_params=pltpu.CompilerParams(vmem_limit_bytes=SMALL),
        name="combine",
    )(in_body, in_over, gates, back)


def partial_kernel(own, two, out):
    out[...] = own[...] + two[...].astype(F32)


def partial_sum(own, two):
    return pl.pallas_call(
        partial_kernel,
        out_shape=jax.ShapeDtypeStruct(two.shape, F32),
        compiler_params=pltpu.CompilerParams(vmem_limit_bytes=SMALL),
        cost_estimate=LONG,
        name="partial_sum",
    )(own, two)


def local(chips, tokens, routes, gates, cotangent, up_weight, down_weight):
    near = 4
    far = chips // near

    def moved(array, hops):
        pairs = []
        for z in range(chips):
            for core in range(CORES):
                to = z * CORES + 1 - core if hops is None else (z + hops(core)) % chips * CORES + core
                pairs.append((z * CORES + core, to))
        return lax.ppermute(array, "dp", pairs)

    routes, gates = routes.T, gates.T
    send, codes = dispatch(routes, gates, tokens, cotangent, up_weight, down_weight)
    codes = lax.all_gather(codes.astype(jnp.float16), "dp").astype(BF16)
    received = lax.all_to_all(send, "expert", split_axis=0, concat_axis=0, tiled=True)
    me = lax.axis_index("dp").astype(jnp.int32)
    place = jnp.stack([me // CORES, me % CORES])
    act, dh, weights, keep, give = expert(place, received, codes)
    got = moved(give, None)

    def total(*arrays):
        return sum(a.astype(F32) for a in arrays)

    got, back = lax.optimization_barrier((got, returns(act, dh, weights)))
    sums = [total(keep[r], got[r]) for r in range(near)]
    two = moved(sums[2].astype(BF16), lambda core: 2 - 4 * core)
    partial = partial_sum(sums[0], two)
    routes, gates, partial = lax.optimization_barrier((routes, gates, partial))
    def both_ways(ahead, behind, steps):
        turn = lambda core: steps * (1 - 2 * core)
        return moved(ahead, turn), moved(behind, lambda core: -turn(core))

    near_sums = both_ways(sums[1].astype(BF16), sums[3].astype(BF16), 1)
    quarter = total(partial, *near_sums).astype(BF16)
    arrived = [
        *both_ways(quarter[1], quarter[3], near),
        moved(quarter[2], lambda core: 2 * near),
    ]
    in_body, in_over = tables(routes)
    back = lax.all_to_all(back, "expert", split_axis=0, concat_axis=0, tiled=True)
    mixed, input_grad = combine(in_body, in_over, gates, back)
    mixed, input_grad, arrived = lax.optimization_barrier((mixed, input_grad, arrived))
    hidden = up_weight.shape[2]
    up_grad, down_grad = (
        total(quarter[0][:, half], *[a[:, half] for a in arrived]).astype(BF16)[None]
        for half in (slice(0, hidden), slice(hidden, 2 * hidden))
    )
    return mixed, input_grad, up_grad, down_grad


def solution(mesh):
    token = P(("dp", "expert"), None)
    weight = P("expert", "dp", None)
    return jax.shard_map(
        functools.partial(local, mesh.shape["dp"] // CORES),
        mesh=mesh,
        in_specs=(token, token, token, token, weight, weight),
        out_specs=(token, token, weight, weight),
        check_vma=False,
    )
```

```python
import functools

import jax
import jax.numpy as jnp
from jax import lax
from jax.experimental import pallas as pl
from jax.experimental.pallas import tpu as pltpu
from jax.sharding import PartitionSpec as P

F32 = jnp.float32
BF16 = jnp.bfloat16
EXPERTS = 16
CAP = 18
BODY = 16
REST = CAP - BODY
BLOCK = 40
CORES = 2
NOTE = 8
SMALL = 16 * 1024 * 1024
LARGE = 40 * 1024 * 1024
WHOLE = 60 * 1024 * 1024
LONG = pl.CostEstimate(flops=50_000_000_000, bytes_accessed=1_000_000, transcendentals=0)


def dot(left, right):
    return lax.dot_general(left, right, (((1,), (0,)), ((), ())), preferred_element_type=F32)


def contract_rows(left, right):
    return lax.dot_general(left, right, (((0,), (0,)), ((), ())), preferred_element_type=F32)


def contract_last(left, right):
    return lax.dot_general(left, right, (((1,), (1,)), ((), ())), preferred_element_type=F32)


def named_and_earlier(routes):
    tokens = routes.shape[1]
    expert = lax.broadcasted_iota(jnp.int32, (EXPERTS, tokens), 0)
    first, second = expert == routes[0:1], expert == routes[1:2]
    earlier = lax.broadcasted_iota(jnp.int32, (tokens, tokens), 0) < lax.broadcasted_iota(
        jnp.int32, (tokens, tokens), 1
    )
    named = jnp.where(first | second, 1.0, 0.0).astype(BF16)
    count = dot(named, jnp.where(earlier, 1.0, 0.0).astype(BF16))
    return first, second, count.astype(jnp.int32)


def slots_of_rows(rows, lanes):
    row = lax.broadcasted_iota(jnp.int32, (1, rows, lanes), 1)
    one = jnp.where(row < BODY, row, -1)
    one = jnp.where((row >= 2 * BODY) & (row < 2 * BODY + REST), row - BODY, one)
    two = jnp.where((row >= BODY) & (row < 2 * BODY), row - BODY, -1)
    two = jnp.where((row >= 2 * BODY + REST) & (row < 2 * BODY + 2 * REST), row - BODY - REST, two)
    return one, two


def coded(weight):
    rows = weight.astype(F32)
    peak = jnp.max(jnp.max(jnp.abs(rows), axis=1, keepdims=True), axis=0, keepdims=True)
    power = jnp.floor(jnp.log2(16384.0 / jnp.maximum(peak, 2.0**-100)))
    factor = jnp.exp2(power).astype(BF16).astype(F32)
    return (rows * factor).astype(BF16), power


def dispatch_kernel(
    routes, gates, up, down, tokens, cotangent, send, codes,
    routes_in, gates_in, up_in, down_in, both, table, rows, small_sems, in_sems, out_sems,
):
    number, width = tokens.shape
    steps, step = rows.shape[:2]
    small = [
        pltpu.make_async_copy(source, target, small_sems.at[k])
        for k, (source, target) in enumerate(
            ((routes, routes_in), (gates, gates_in), (up, up_in), (down, down_in))
        )
    ]
    large = [
        pltpu.make_async_copy(source, both.at[pl.ds(k * number, number)], in_sems.at[k])
        for k, source in enumerate((tokens, cotangent))
    ]
    for load in small + large:
        load.start()
    for load in small:
        load.wait()
    share, hidden = up.shape[1:]
    codes[:share], up_power = coded(up_in[0])
    codes[share : 2 * share], down_power = coded(down_in[0])
    note = lax.broadcasted_iota(jnp.int32, (NOTE, hidden), 0) < NOTE // 2
    codes[2 * share :] = jnp.where(note, up_power, down_power).astype(BF16)
    first, second, count = named_and_earlier(routes_in[...])
    held = jnp.where(first | second, count, -2)[:, None, :]
    one, two = slots_of_rows(BLOCK, number)
    gate = jnp.where(first, gates_in[0:1], 0.0) + jnp.where(second, gates_in[1:2], 0.0)
    in_one, in_two = held == one, held == two
    table[:, :number] = jnp.where(in_one, 1.0, 0.0).reshape(EXPERTS * BLOCK, number).astype(BF16)
    table[:, number:] = jnp.where(in_two, 1.0, 0.0).reshape(EXPERTS * BLOCK, number).astype(BF16)
    scale = jnp.where(in_two, gate[:, None, :], 0.0) + jnp.where(in_one, 1.0, 0.0)
    scale = jnp.sum(scale.reshape(EXPERTS * BLOCK, number), axis=1, keepdims=True)
    for load in large:
        load.wait()
    stores = []
    for k in range(steps):
        at = slice(k * step * BLOCK, (k + 1) * step * BLOCK)
        block = dot(table[at], both[...]) * scale[at]
        rows[k] = block.astype(BF16).reshape(step, BLOCK, width)
        stores.append(
            pltpu.make_async_copy(rows.at[k], send.at[pl.ds(k * step, step)], out_sems.at[k])
        )
        stores[-1].start()
    for store in stores:
        store.wait()


def dispatch(routes, gates, tokens, cotangent, up_weight, down_weight):
    number, width = tokens.shape
    share, hidden = up_weight.shape[1:]
    step = 4
    steps = EXPERTS // step
    anywhere = pl.BlockSpec(memory_space=pl.ANY)
    return pl.pallas_call(
        dispatch_kernel,
        in_specs=[anywhere] * 6,
        out_specs=[anywhere, pl.BlockSpec(memory_space=pltpu.VMEM)],
        out_shape=[
            jax.ShapeDtypeStruct((EXPERTS, BLOCK, width), BF16),
            jax.ShapeDtypeStruct((2 * share + NOTE, hidden), BF16),
        ],
        scratch_shapes=[
            pltpu.VMEM(routes.shape, jnp.int32),
            pltpu.VMEM(gates.shape, F32),
            pltpu.VMEM(up_weight.shape, BF16),
            pltpu.VMEM(down_weight.shape, BF16),
            pltpu.VMEM((2 * number, width), BF16),
            pltpu.VMEM((EXPERTS * BLOCK, 2 * number), BF16),
            pltpu.VMEM((steps, step, BLOCK, width), BF16),
            pltpu.SemaphoreType.DMA((4,)),
            pltpu.SemaphoreType.DMA((2,)),
            pltpu.SemaphoreType.DMA((steps,)),
        ],
        compiler_params=pltpu.CompilerParams(vmem_limit_bytes=WHOLE),
        name="dispatch",
    )(routes, gates, up_weight, down_weight, tokens, cotangent)


def ones_where(rows, columns, chosen):
    row = lax.broadcasted_iota(jnp.int32, (rows, columns), 0)
    column = lax.broadcasted_iota(jnp.int32, (rows, columns), 1)
    return jnp.where(chosen(row) == column, 1.0, 0.0).astype(BF16)


def decode_kernel(codes, weights):
    width, hidden = weights.shape[0], codes.shape[2]
    share = (codes.shape[1] - NOTE) // 2
    factor = jnp.exp2(-codes[:, 2 * share :, :].astype(F32)).astype(BF16)
    for n in range(2):
        rows = codes[:, n * share : (n + 1) * share, :]
        here = factor[:, n * NOTE // 2 : n * NOTE // 2 + 1, :]
        weights[:, n * hidden : (n + 1) * hidden] = (rows * here).reshape(width, hidden)


def decode(codes):
    devices, rows, hidden = codes.shape
    return pl.pallas_call(
        decode_kernel,
        out_shape=jax.ShapeDtypeStruct((devices * (rows - NOTE) // 2, 2 * hidden), BF16),
        compiler_params=pltpu.CompilerParams(vmem_limit_bytes=LARGE),
        name="decode",
    )(codes)


def expert_kernel(
    place, received, weights, act_out, dh_out, keep, give, x, g
):
    width = received.shape[2]
    hidden = weights.shape[1] // 2
    share = keep.shape[2]
    body = EXPERTS * BODY
    rest = EXPERTS * REST
    x[:body] = received[:, :BODY, :].reshape(body, width)
    g[:body] = received[:, BODY : 2 * BODY, :].reshape(body, width)
    eight = BLOCK - 2 * BODY
    over = received[:, 2 * BODY :, :].reshape(EXPERTS * eight, width)
    pick = ones_where(
        2 * rest,
        EXPERTS * eight,
        lambda row: (row % rest) // REST * eight + row // rest * REST + row % REST,
    )
    over = dot(pick, over).astype(BF16)
    x[body:] = over[:rest]
    g[body:] = over[rest:]
    hpre = dot(x[...], weights[:, :hidden])
    dact = dot(g[...], weights[:, hidden:])
    s = 1.0 / (1.0 + jnp.exp(-hpre))
    act = (hpre * s).astype(BF16)
    dh = (dact * s * (1.0 + hpre * (1.0 - s))).astype(BF16)
    act_out[...] = act
    dh_out[...] = dh
    near, far = keep.shape[:2]
    z, mine = place[0], place[1]
    step = 512
    each = step // (CORES * share)

    def parts_of(core):
        for k in range(width // step):
            rows = slice(k * step, (k + 1) * step)
            halves = (
                contract_rows(x[:, rows], dh).astype(BF16),
                contract_rows(g[:, rows], act).astype(BF16),
            )
            for n in range(each):
                away = lax.rem(k * each + n - z + near * far, near * far)
                r = lax.rem(away, near)
                for owner, out in ((core, keep), (1 - core, give)):
                    later = jnp.where(r == 3, 1, jnp.where(r == 2, owner, 0))
                    j = lax.rem(away // near + later, far)
                    to = (r, j)
                    if owner == 1:
                        to = (lax.rem(near - r, near), lax.rem(far - j, far))
                    at = slice((n * CORES + owner) * share, (n * CORES + owner + 1) * share)
                    out[(*to, slice(None), slice(0, hidden))] = halves[0][at]
                    out[(*to, slice(None), slice(hidden, 2 * hidden))] = halves[1][at]

    for core in range(CORES):
        pl.when(mine == core)(functools.partial(parts_of, core))


def expert(place, received, weights, share):
    width, wide = weights.shape
    rows = EXPERTS * CAP
    whole = pl.BlockSpec(memory_space=pltpu.VMEM)
    chips = width // share // CORES
    near = 4
    return pl.pallas_call(
        expert_kernel,
        in_specs=[pl.BlockSpec(memory_space=pltpu.SMEM), whole, whole],
        out_specs=[whole] * 4,
        out_shape=[
            jax.ShapeDtypeStruct((rows, wide // 2), BF16),
            jax.ShapeDtypeStruct((rows, wide // 2), BF16),
            jax.ShapeDtypeStruct((near, chips // near, share, wide), BF16),
            jax.ShapeDtypeStruct((near, chips // near, share, wide), BF16),
        ],
        scratch_shapes=[
            pltpu.VMEM((rows, width), BF16),
            pltpu.VMEM((rows, width), BF16),
        ],
        compiler_params=pltpu.CompilerParams(vmem_limit_bytes=LARGE),
        name="expert",
    )(place, received, weights)


def return_kernel(act, dh, weights, back):
    hidden = weights.shape[1] // 2
    half = weights.shape[0] // 2
    body = EXPERTS * BODY
    rest = EXPERTS * REST
    over = []
    for kind, value in enumerate((act, dh)):
        for side in range(2):
            at = (2 * kind + side) * BODY
            weight = weights[side * half : (side + 1) * half, (1 - kind) * hidden : (2 - kind) * hidden]
            rows = contract_last(value[...], weight).astype(BF16)
            back[:, at : at + BODY, :] = rows[:body].reshape(EXPERTS, BODY, half)
            over.append(rows[body:])
    eight = 4 * REST
    spread = ones_where(
        EXPERTS * eight,
        4 * rest,
        lambda row: row % eight // REST * rest + row // eight * REST + row % REST,
    )
    over = dot(spread, jnp.concatenate(over, axis=0)).astype(BF16)
    back[:, 4 * BODY :, :] = over.reshape(EXPERTS, eight, half)


def returns(act, dh, weights):
    whole = pl.BlockSpec(memory_space=pltpu.VMEM)
    return pl.pallas_call(
        return_kernel,
        in_specs=[whole] * 3,
        out_specs=whole,
        out_shape=jax.ShapeDtypeStruct((EXPERTS, 4 * CAP, weights.shape[0] // 2), BF16),
        compiler_params=pltpu.CompilerParams(vmem_limit_bytes=LARGE),
        cost_estimate=LONG,
        name="returns",
    )(act, dh, weights)


def table_kernel(routes, body, over):
    number = routes.shape[1]
    first, second, count = named_and_earlier(routes[...])
    slot = lax.broadcasted_iota(jnp.int32, (1, BODY, number), 1)
    place = lax.broadcasted_iota(jnp.int32, (1, 4 * REST, number), 1)
    for k, chosen in enumerate((first, second, first | second)):
        held = jnp.where(chosen, count, -2)[:, None, :]
        at = slice(k * number, (k + 1) * number)
        here = jnp.where(held == slot, 1.0, 0.0).reshape(EXPERTS * BODY, number)
        body[at] = here.T.astype(BF16)
        for side in range(2):
            start = REST * (2 * (k // 2) + side)
            mine = (place >= start) & (place < start + REST)
            here = jnp.where(mine & (held == place - start + BODY), 1.0, 0.0)
            over[side, at] = here.reshape(EXPERTS * 4 * REST, number).T.astype(BF16)


def tables(routes):
    number = routes.shape[1]
    return pl.pallas_call(
        table_kernel,
        out_shape=[
            jax.ShapeDtypeStruct((3 * number, EXPERTS * BODY), BF16),
            jax.ShapeDtypeStruct((2, 3 * number, EXPERTS * 4 * REST), BF16),
        ],
        compiler_params=pltpu.CompilerParams(vmem_limit_bytes=SMALL),
        name="tables",
    )(routes)


def combine_kernel(in_body, in_over, gates, back, mixed, input_grad):
    number = mixed.shape[0]
    half = back.shape[2]
    here = lax.broadcasted_iota(jnp.int32, (number, number), 0) == lax.broadcasted_iota(
        jnp.int32, (number, number), 1
    )
    gate = [
        jnp.sum(jnp.where(here, gates[k : k + 1], 0.0), axis=1, keepdims=True) for k in range(2)
    ]
    over = back[:, 4 * BODY :, :].reshape(EXPERTS * 4 * REST, half)

    def picked(at, kind, side):
        body = back[:, (2 * kind + side) * BODY : (2 * kind + side + 1) * BODY, :]
        return dot(
            jnp.concatenate([in_body[at], in_over[side, at]], axis=1),
            jnp.concatenate([body.reshape(EXPERTS * BODY, half), over], axis=0),
        )

    for side in range(2):
        columns = slice(side * half, (side + 1) * half)
        pairs = picked(slice(0, 2 * number), 0, side)
        mixed[:, columns] = (gate[0] * pairs[:number] + gate[1] * pairs[number:]).astype(BF16)
        input_grad[:, columns] = picked(slice(2 * number, 3 * number), 1, side).astype(BF16)


def combine(in_body, in_over, gates, back):
    number = gates.shape[1]
    width = 2 * back.shape[2]
    return pl.pallas_call(
        combine_kernel,
        out_shape=[jax.ShapeDtypeStruct((number, width), BF16)] * 2,
        compiler_params=pltpu.CompilerParams(vmem_limit_bytes=SMALL),
        name="combine",
    )(in_body, in_over, gates, back)


def partial_kernel(own, two, out):
    out[...] = own[...] + two[...].astype(F32)


def partial_sum(own, two):
    return pl.pallas_call(
        partial_kernel,
        out_shape=jax.ShapeDtypeStruct(two.shape, F32),
        compiler_params=pltpu.CompilerParams(vmem_limit_bytes=SMALL),
        cost_estimate=LONG,
        name="partial_sum",
    )(own, two)


def local(chips, tokens, routes, gates, cotangent, up_weight, down_weight):
    near = 4
    far = chips // near

    def moved(array, hops):
        pairs = []
        for z in range(chips):
            for core in range(CORES):
                to = z * CORES + 1 - core if hops is None else (z + hops(core)) % chips * CORES + core
                pairs.append((z * CORES + core, to))
        return lax.ppermute(array, "dp", pairs)

    routes, gates = routes.T, gates.T
    send, codes = dispatch(routes, gates, tokens, cotangent, up_weight, down_weight)
    codes = lax.all_gather(codes.astype(jnp.float16), "dp").astype(BF16)
    received = lax.all_to_all(send, "expert", split_axis=0, concat_axis=0, tiled=True)
    me = lax.axis_index("dp").astype(jnp.int32)
    place = jnp.stack([me // CORES, me % CORES])
    weights = decode(codes)
    act, dh, keep, give = expert(place, received, weights, up_weight.shape[1])
    got = moved(give, None)

    def total(*arrays):
        return sum(a.astype(F32) for a in arrays)

    got, back = lax.optimization_barrier((got, returns(act, dh, weights)))
    sums = [total(keep[r], got[r]) for r in range(near)]
    two = moved(sums[2].astype(BF16), lambda core: 2 - 4 * core)
    partial = partial_sum(sums[0], two)
    routes, gates, partial = lax.optimization_barrier((routes, gates, partial))
    def both_ways(ahead, behind, steps):
        turn = lambda core: steps * (1 - 2 * core)
        return moved(ahead, turn), moved(behind, lambda core: -turn(core))

    near_sums = both_ways(sums[1].astype(BF16), sums[3].astype(BF16), 1)
    quarter = total(partial, *near_sums).astype(BF16)
    arrived = [
        *both_ways(quarter[1], quarter[3], near),
        moved(quarter[2], lambda core: 2 * near),
    ]
    in_body, in_over = tables(routes)
    back = lax.all_to_all(back, "expert", split_axis=0, concat_axis=0, tiled=True)
    mixed, input_grad = combine(in_body, in_over, gates, back)
    mixed, input_grad, arrived = lax.optimization_barrier((mixed, input_grad, arrived))
    hidden = up_weight.shape[2]
    up_grad, down_grad = (
        total(quarter[0][:, half], *[a[:, half] for a in arrived]).astype(BF16)[None]
        for half in (slice(0, hidden), slice(hidden, 2 * hidden))
    )
    return mixed, input_grad, up_grad, down_grad


def solution(mesh):
    token = P(("dp", "expert"), None)
    weight = P("expert", "dp", None)
    return jax.shard_map(
        functools.partial(local, mesh.shape["dp"] // CORES),
        mesh=mesh,
        in_specs=(token, token, token, token, weight, weight),
        out_specs=(token, token, weight, weight),
        check_vma=False,
    )
```
